256 devices in a mesh: row: 8 (over z_hi, core), col: 32 (over z_lo, x, y).
Axes of the slice: x: 4, y: 4, z: 8 (z_hi: 4, z_lo: 2; z = z_hi * 2 + z_lo), core: 2. Of those that a mesh axis runs over, the one named last changes fastest.
Arguments:
- features: float32 [32, 1024, 128], P('col', 'row'), may hold values from -6 to 6
- block_values: float32 [8, 32, 160, 128, 128], P('row', 'col'), may hold values from -0.0390625 to 0.0390625
- block_rows: int32 [8, 32, 160], P('row', 'col'), may hold values from 0 to 31
- block_cols: int32 [8, 32, 160], P('row', 'col'), may hold values from 0 to 7
- live_block_count: int32 [8, 32], P('row', 'col'), may hold values from 1 to 160, as said below
- weight: float32 [128, 128], replicated, may hold values from -0.5 to 0.5
- cotangent: float32 [8, 4096, 128], P('row', 'col'), may hold values from -6 to 6
Outputs:
- activated: float32 [8, 4096, 128], P('row', 'col')
- weight_grad: float32 [128, 128], replicated
- feature_grad: float32 [32, 1024, 128], P('col', 'row')
The draws below stay inside these ranges and needn't reach their ends.
Inputs may be any that keep to these rules, and one draw needn't show every extreme that they name: `live_block_count`: some tile has all 160 slots live.
All inputs are finite; a program needn't handle non-finite values.
Results may differ from the reference program's by a relative error of at most 0.0003.
Values sent between devices are 32-bit elements; how exact they have to be, the bound alone decides.
A program may use at most 128 MiB of HBM per device.

```python
import jax
import jax.numpy as jnp
from jax import lax

F = 128
BS = 128
SUB = 128
NB = 160
NODES = 32768
TROWB = 32
TCOLB = 8
N_ROW = 8
N_COL = 32


def draw_live_block_count(key, part):
    key = jax.random.fold_in(key, 7)
    first_key, second_key = jax.random.split(key)
    spread_rows = jax.random.randint(first_key, (N_ROW * N_COL,), 0, 1000, dtype=jnp.int32)
    counts = 1 + (NB - 1) * (spread_rows * spread_rows) // 1000000
    picked = jax.random.randint(second_key, (), 0, N_ROW * N_COL, dtype=jnp.int32)
    place = jnp.arange(N_ROW * N_COL, dtype=jnp.int32)
    counts = jnp.where(place == picked, NB, counts)
    return counts.reshape(N_ROW, N_COL).astype(jnp.int32)


def touch_ends(result, rng, low, top_value):
    longest = result.shape.index(max(result.shape))
    spots = []
    for shift in (0, 1):
        where = [jax.random.randint(jax.random.fold_in(rng, axis), (), 0, length) for axis, length in enumerate(result.shape)]
        where[longest] = (where[longest] + shift) % result.shape[longest]
        spots.append(tuple(where))
    return result.at[spots[0]].set(low).at[spots[1]].set(top_value)


def shard_levels(stream_key, dims, cuts, smallest, largest):
    level = 1.0
    for dim, blocks in cuts:
        steps = jax.random.uniform(jax.random.fold_in(jax.random.fold_in(stream_key, 6), dim), (blocks,), jnp.float32, smallest / len(cuts), largest / len(cuts))
        level = level * jnp.repeat(jnp.exp(steps), dims[dim] // blocks).reshape((-1,) + (1,) * (len(dims) - 1 - dim))
    return level


def centred(own_key, extent, spread, most, pieces=(), held_as=jnp.bfloat16):
    loudness = shard_levels(own_key, extent, pieces, -0.22, 0.18) if pieces else 1.0
    result = jax.random.normal(own_key, extent, jnp.float32) * spread * loudness
    return jnp.minimum(jnp.maximum(result, -most), most).astype(held_as)


def setup_inputs(seed: int = 0) -> dict:
    keys = jax.random.split(jax.random.key(seed), 8)
    features = centred(keys[0], (N_COL, N_ROW * SUB, F), 1.0, 6.0, ((0, 32), (1, 8)), jnp.float32)
    block_values = centred(keys[1], (N_ROW, N_COL, NB, BS, BS), (NB * BS * BS // SUB) ** -0.5, 0.0390625, ((0, 8), (1, 32)), jnp.float32)
    block_rows = touch_ends(jax.random.randint(keys[2], (N_ROW, N_COL, NB), 0, TROWB), jax.random.fold_in(keys[2], 1), 0, TROWB - 1).astype(jnp.int32)
    block_cols = touch_ends(jax.random.randint(keys[3], (N_ROW, N_COL, NB), 0, TCOLB), jax.random.fold_in(keys[3], 1), 0, TCOLB - 1).astype(jnp.int32)
    live_block_count = draw_live_block_count(jax.random.fold_in(keys[7], 71), 0)
    weight = centred(keys[5], (F, F), F ** -0.5, 0.5, (), jnp.float32)
    cotangent = centred(keys[6], (N_ROW, N_COL * SUB, F), 1.0, 6.0, ((0, 8), (1, 32)), jnp.float32)
    return dict(features=features, block_values=block_values, block_rows=block_rows, block_cols=block_cols, live_block_count=live_block_count, weight=weight, cotangent=cotangent)


def silu_grad(z_vals):
    sig = jax.nn.sigmoid(z_vals)
    return sig * (1.0 + z_vals * (1.0 - sig))

def reference(features, block_values, block_rows, block_cols, live_block_count, weight, cotangent):
    tiles = N_ROW * N_COL
    vals_flat = block_values.reshape(tiles, NB, BS, BS)
    rows_flat = block_rows.reshape(tiles, NB)
    flattened_columns = block_cols.reshape(tiles, NB)
    count_flat = live_block_count.reshape(tiles)
    tile_index = jnp.arange(tiles, dtype=jnp.int32)
    tile_r = tile_index // N_COL
    tile_c = tile_index % N_COL
    slot_index = jnp.arange(NB, dtype=jnp.int32)
    xblocks = features.reshape(N_COL * TCOLB, BS, F)
    hp = lax.Precision.HIGHEST

    def forward_tile(total, items):
        entry_values, brows, bcols, count, rpos, cpos = items
        is_live_slot = (slot_index < count).astype(jnp.float32)
        chosen = xblocks[(cpos * TCOLB + bcols).astype(jnp.int32)]
        prods = jnp.einsum('kij,kjf->kif', entry_values, chosen, precision=hp) * is_live_slot[:, None, None]
        total = total.at[(rpos * TROWB + brows).astype(jnp.int32)].add(prods)
        return (total, None)
    start = jnp.zeros((N_ROW * TROWB, BS, F), jnp.float32)
    yblocks, _ = lax.scan(forward_tile, start, (vals_flat, rows_flat, flattened_columns, count_flat, tile_r, tile_c))
    y_all = yblocks.reshape(NODES, F)
    z_all = jnp.dot(y_all, weight, precision=hp, preferred_element_type=jnp.float32)
    activated = jax.nn.silu(z_all)
    grads = cotangent.reshape(NODES, F)
    dz_all = grads * silu_grad(z_all)
    weight_grad = jnp.dot(y_all.T, dz_all, precision=hp, preferred_element_type=jnp.float32)
    pblocks = jnp.dot(dz_all, weight.T, precision=hp, preferred_element_type=jnp.float32).reshape(N_ROW * TROWB, BS, F)

    def reverse_tile_step(total, items):
        entry_values, brows, bcols, count, rpos, cpos = items
        is_live_slot = (slot_index < count).astype(jnp.float32)
        chosen = pblocks[(rpos * TROWB + brows).astype(jnp.int32)]
        prods = jnp.einsum('kji,kjf->kif', entry_values, chosen, precision=hp) * is_live_slot[:, None, None]
        total = total.at[(cpos * TCOLB + bcols).astype(jnp.int32)].add(prods)
        return (total, None)
    start_back = jnp.zeros((N_COL * TCOLB, BS, F), jnp.float32)
    xgrad, _ = lax.scan(reverse_tile_step, start_back, (vals_flat, rows_flat, flattened_columns, count_flat, tile_r, tile_c))
    return (activated.reshape(N_ROW, N_COL * SUB, F), weight_grad, xgrad.reshape(N_COL, N_ROW * SUB, F))
```

```python
import functools

import jax
import jax.numpy as jnp
from jax import lax
from jax.experimental import pallas as pl
from jax.experimental.pallas import tpu as pltpu
from jax.sharding import PartitionSpec as P

B = 128
SLOTS = 160
COLS = 8
PEERS = 32
ROWS = 8
XY = 16
CHUNK = 20
CHUNKS = SLOTS // CHUNK
F32 = jnp.float32
BF16 = jnp.bfloat16
HP = lax.Precision.HIGHEST


def split(v):
    hi = v.astype(BF16)
    return hi, (v - hi.astype(F32)).astype(BF16)


def kernel(
    prev, idx, feat, weight, cot, values,
    act_out, wgrad_out, fgrad_out,
    land, summed, pieces, xbuf, xx, ysend, yrecv, ysum, pown, precv, facc, srecv, zsend, zrecv,
    wterm, w1, w2, w3,
    asem, xs, xr, ys, yr, ps, pr, ss, sr, zs, zr, w1s, w1r, w2s, w2r, w3s, w3r,
):
    r = lax.axis_index("row")
    c = lax.axis_index("col")
    zh, core = lax.div(r, 2), lax.rem(r, 2)
    zl, x, y = lax.div(c, 16), lax.rem(lax.div(c, 4), 4), lax.rem(c, 4)
    xy = lax.rem(c, XY)
    sib = zh * 2 + (1 - core)

    def col_at(d):
        return (
            lax.rem(zl + lax.div(d, 16), 2) * 16
            + lax.rem(x + lax.rem(lax.div(d, 4), 4), 4) * 4
            + lax.rem(y + lax.rem(d, 4), 4)
        )

    def col_from(d):
        return (
            lax.rem(zl + lax.div(d, 16), 2) * 16
            + lax.rem(x + 4 - lax.rem(lax.div(d, 4), 4), 4) * 4
            + lax.rem(y + 4 - lax.rem(d, 4), 4)
        )

    def to(src, dst, send, recv, row, col):
        return pltpu.make_async_remote_copy(
            src_ref=src, dst_ref=dst, send_sem=send, recv_sem=recv,
            device_id={"row": row, "col": col}, device_id_type=pl.DeviceIdType.MESH,
        )

    def loads(i):
        part = pl.ds(i * CHUNK, CHUNK)
        return pltpu.make_async_copy(values.at[part], land.at[part], asem.at[i])

    for i in range(CHUNKS):
        loads(i).start()

    barrier = pltpu.get_barrier_semaphore()

    @pl.loop(1, PEERS)
    def _(d):
        pl.semaphore_signal(barrier, 1, device_id={"row": r, "col": col_at(d)}, device_id_type=pl.DeviceIdType.MESH)

    @pl.loop(1, ROWS)
    def _(e):
        pl.semaphore_signal(barrier, 1, device_id={"row": lax.rem(r + e, ROWS), "col": c}, device_id_type=pl.DeviceIdType.MESH)

    pl.semaphore_wait(barrier, PEERS - 1 + ROWS - 1)

    def xcopy(src, slot, send, row):
        return to(src, xbuf.at[slot], xs.at[send], xr.at[slot], row, c)

    for dz in range(1, 4):
        xcopy(feat, r, dz, lax.rem(zh + dz, 4) * 2 + core).start()
    xcopy(feat, r, 0, sib).start()
    xbuf[r] = feat[...]

    summed[SLOTS] = jnp.zeros((B, B), F32)
    pieces[SLOTS] = jnp.zeros((B, 2 * B), BF16)

    def prepare(i):
        loads(i).wait()

        @pl.loop(i * CHUNK, (i + 1) * CHUNK)
        def _(k):
            v = land[k] + summed[prev[k]]
            summed[k] = v
            hi, lo = split(v)
            pieces[k, :, :B] = hi
            pieces[k, :, B:] = lo

    for i in range(CHUNKS // 2):
        prepare(i)

    for dz in range(1, 4):
        slot = lax.rem(zh + 4 - dz, 4) * 2 + core
        xcopy(feat, slot, dz, sib).wait_recv()
        xcopy(xbuf.at[slot], slot, 3 + dz, sib).start()

    for i in range(CHUNKS // 2, CHUNKS):
        prepare(i)

    for dz in range(4):
        slot = lax.rem(zh + dz, 4) * 2 + (1 - core)
        xcopy(feat, slot, 0, sib).wait_recv()
    for i in range(COLS):
        hi, lo = split(xbuf[i])
        xx[i, :B, :B] = hi
        xx[i, B:, :B] = hi
        xx[i, :B, B:] = lo
        xx[i, B:, B:] = lo

    def y_block(at):
        acc = jnp.zeros((B, 2 * B), F32)
        for i in range(COLS):
            acc = acc + jnp.dot(pieces[idx[at * COLS + i]], xx[i], preferred_element_type=F32)
        return acc[:, :B] + acc[:, B:]

    def ycopy(d):
        return to(ysend.at[d], yrecv.at[d], ys.at[d], yr.at[d], r, col_at(d))

    @pl.loop(1, PEERS)
    def _(d):
        ysend[d] = y_block(col_at(d))
        ycopy(d).start()

    ysum[...] = y_block(c)

    @pl.loop(1, PEERS)
    def _(d):
        ycopy(d).wait_recv()
        ysum[...] += yrecv[d]

    yv = ysum[...]
    w = weight[...]
    z = jnp.dot(yv, w, precision=HP, preferred_element_type=F32)
    s = jax.nn.sigmoid(z)
    act_out[...] = z * s
    dz_vals = cot[...] * (s * (1.0 + z * (1.0 - s)))
    p_t = lax.dot_general(w, dz_vals, (((1,), (1,)), ((), ())), precision=HP, preferred_element_type=F32)
    pown[...] = p_t
    precv[0] = p_t

    def pcopy(d):
        return to(pown, precv.at[d], ps.at[d], pr.at[d], r, col_at(d))

    @pl.loop(1, PEERS)
    def _(d):
        pcopy(d).start()

    term = lax.dot_general(yv, dz_vals, (((0,), (0,)), ((), ())), precision=HP, preferred_element_type=F32)
    wterm[...] = term.reshape(XY, 8, B)

    def w1copy(d, owner, source):
        return to(wterm.at[lax.rem(owner, XY)], w1.at[source], w1s.at[d], w1r.at[source], r, owner)

    @pl.loop(1, PEERS)
    def _(d):
        w1copy(d, col_at(d), c).start()

    w1[c] = wterm[xy]

    for i in range(COLS):
        facc[i] = jnp.zeros((B, B), F32)

    def back(j):
        s1, s2 = col_from(2 * j), col_from(2 * j + 1)
        p = jnp.concatenate([precv[2 * j], precv[2 * j + 1]], axis=1)
        hi, lo = split(p)
        lhs = jnp.concatenate([hi, lo], axis=0)
        for i in range(COLS):
            rhs = jnp.concatenate([pieces[idx[s1 * COLS + i]], pieces[idx[s2 * COLS + i]]], axis=0)
            res = jnp.dot(lhs, rhs, preferred_element_type=F32)
            facc[i] += (res[:B, :B] + res[B:, B:]) + (res[:B, B:] + res[B:, :B])

    def back_pairs(lo, hi):
        @pl.loop(lo, hi)
        def _(j):
            pcopy(2 * j).wait_recv()
            pcopy(2 * j + 1).wait_recv()
            back(j)

    pcopy(1).wait_recv()
    back(0)
    back_pairs(1, 12)

    @pl.loop(1, PEERS)
    def _(d):
        w1copy(d, c, col_from(d)).wait_recv()

    w2[r] = jnp.sum(w1[...], axis=0)

    def w2copy(e, row, source):
        return to(w2.at[r], w2.at[source], w2s.at[e], w2r.at[source], row, c)

    @pl.loop(1, ROWS)
    def _(e):
        w2copy(e, lax.rem(r + e, ROWS), r).start()

    back_pairs(12, 14)

    @pl.loop(1, ROWS)
    def _(e):
        w2copy(e, r, lax.rem(r + ROWS - e, ROWS)).wait_recv()

    w3[xy] = jnp.sum(w2[...], axis=0)

    def w3copy(d, col, source):
        return to(w3.at[xy], w3.at[source], w3s.at[d], w3r.at[source], r, col)

    @pl.loop(1, XY)
    def _(d):
        w3copy(d, col_at(d), xy).start()

    back_pairs(14, 16)

    def scopy(q):
        return to(facc.at[q * 2 + (1 - core)], srecv.at[q], ss.at[q], sr.at[q], sib, c)

    def zcopy(d):
        return to(zsend.at[d], zrecv.at[d], zs.at[d], zr.at[d], lax.rem(zh + d, 4) * 2 + core, c)

    order = [lax.rem(zh + d, 4) for d in (1, 3, 2, 0)]
    for q in order:
        scopy(q).start()
    for d, q in zip((1, 3, 2), order):
        scopy(q).wait_recv()
        zsend[d] = facc[q * 2 + core] + srecv[q]
        zcopy(d).start()
    scopy(zh).wait_recv()
    total = facc[r] + srecv[zh]

    @pl.loop(1, XY)
    def _(d):
        w3copy(d, c, lax.rem(col_from(d), XY)).wait_recv()

    wgrad_out[...] = w3[...].reshape(B, B)

    for d in (1, 3, 2):
        zcopy(d).wait_recv()
        total = total + zrecv[d]
    fgrad_out[...] = total.T

    for dz in range(1, 4):
        xcopy(feat, r, dz, sib).wait_send()
        xcopy(feat, r, 3 + dz, sib).wait_send()
        zcopy(dz).wait_send()
    xcopy(feat, r, 0, sib).wait_send()
    for q in order:
        scopy(q).wait_send()

    @pl.loop(1, PEERS)
    def _(d):
        ycopy(d).wait_send()
        pcopy(d).wait_send()
        w1copy(d, c, c).wait_send()

    @pl.loop(1, ROWS)
    def _(e):
        w2copy(e, r, r).wait_send()

    @pl.loop(1, XY)
    def _(d):
        w3copy(d, c, xy).wait_send()


def local(features, block_values, block_rows, block_cols, live_block_count, weight, cotangent):
    slot = jnp.arange(SLOTS, dtype=jnp.int32)
    live = slot < live_block_count[0, 0]
    position = jnp.where(live, block_rows[0, 0] * COLS + block_cols[0, 0], -1)

    def last(match):
        return jnp.max(jnp.where(match, slot[None, :] + 1, 0), axis=1)

    prev = last((position[None, :] == position[:, None]) & (slot[None, :] < slot[:, None]) & live[None, :])
    idx = last(position[None, :] == jnp.arange(PEERS * COLS, dtype=jnp.int32)[:, None])
    prev = jnp.where(prev > 0, prev - 1, SLOTS)
    idx = jnp.where(idx > 0, idx - 1, SLOTS)

    vmem = pl.BlockSpec(memory_space=pltpu.VMEM)
    smem = pl.BlockSpec(memory_space=pltpu.SMEM)
    dma = pltpu.SemaphoreType.DMA
    act, wgrad, fgrad = pl.pallas_call(
        kernel,
        out_shape=[jax.ShapeDtypeStruct((B, B), F32)] * 3,
        in_specs=[smem, smem, vmem, vmem, vmem, pl.BlockSpec(memory_space=pl.ANY)],
        out_specs=[vmem, vmem, vmem],
        scratch_shapes=[
            pltpu.VMEM((SLOTS, B, B), F32),
            pltpu.VMEM((SLOTS + 1, B, B), F32),
            pltpu.VMEM((SLOTS + 1, B, 2 * B), BF16),
            pltpu.VMEM((COLS, B, B), F32),
            pltpu.VMEM((COLS, 2 * B, 2 * B), BF16),
            pltpu.VMEM((PEERS, B, B), F32),
            pltpu.VMEM((PEERS, B, B), F32),
            pltpu.VMEM((B, B), F32),
            pltpu.VMEM((B, B), F32),
            pltpu.VMEM((PEERS, B, B), F32),
            pltpu.VMEM((COLS, B, B), F32),
            pltpu.VMEM((4, B, B), F32),
            pltpu.VMEM((4, B, B), F32),
            pltpu.VMEM((4, B, B), F32),
            pltpu.VMEM((XY, 8, B), F32),
            pltpu.VMEM((PEERS, 8, B), F32),
            pltpu.VMEM((ROWS, 8, B), F32),
            pltpu.VMEM((XY, 8, B), F32),
            dma((CHUNKS,)),
            dma((7,)),
            dma((ROWS,)),
            dma((PEERS,)),
            dma((PEERS,)),
            dma((PEERS,)),
            dma((PEERS,)),
            dma((4,)),
            dma((4,)),
            dma((4,)),
            dma((4,)),
            dma((PEERS,)),
            dma((PEERS,)),
            dma((ROWS,)),
            dma((ROWS,)),
            dma((XY,)),
            dma((XY,)),
        ],
        compiler_params=pltpu.CompilerParams(
            collective_id=0, has_side_effects=True, vmem_limit_bytes=56 * 1024 * 1024
        ),
    )(prev, idx, features[0], weight, cotangent[0], block_values[0, 0])
    return act[None], wgrad, fgrad[None]


def solution(mesh):
    in_specs = (
        P("col", "row", None),
        P("row", "col", None, None, None),
        P("row", "col", None),
        P("row", "col", None),
        P("row", "col"),
        P(),
        P("row", "col", None),
    )
    out_specs = (P("row", "col", None), P(), P("col", "row", None))
    return jax.shard_map(local, mesh=mesh, in_specs=in_specs, out_specs=out_specs, check_vma=False)
```

```python
import jax
import jax.numpy as jnp
from jax import lax
from jax.experimental import pallas as pl
from jax.experimental.pallas import tpu as pltpu
from jax.sharding import PartitionSpec as P

B = 128
SLOTS = 160
COLS = 8
CHUNK = 20
CHUNKS = SLOTS // CHUNK
WIDE = 256
F32 = jnp.float32
BF16 = jnp.bfloat16
HP = lax.Precision.HIGHEST


def split(v):
    hi = v.astype(BF16)
    return hi, (v - hi.astype(F32)).astype(BF16)


def kernel(
    count, rows, cols, feat, weight, cot, values,
    act_out, wgrad_out, fgrad_out,
    land, summed, pieces, posbuf, tabv, tab, xbuf, xx, cotbuf, ysend, yrecv, y2send, y2recv,
    plane, zplane, acts, pbuf, facc, srecv, zsend, zrecv,
    wterm, wa, wsum, wb, wc, wd, wz, wg,
    asem, tsem, xs, xr, cs, cr, ys, yr, y2s, y2r, es, er, ps, pr, ss, sr, zs, zr,
    was, war, wbs, wbr, wds, wdr, wzs, wzr, wys, wyr, wxs, wxr,
):
    r = lax.axis_index("row")
    c = lax.axis_index("col")
    zh, core = lax.div(r, 2), lax.rem(r, 2)
    zl, x, y = lax.div(c, 16), lax.rem(lax.div(c, 4), 4), lax.rem(c, 4)
    sib = zh * 2 + (1 - core)

    def plus(v, d):
        return lax.rem(v + d, 4)

    def col(h, at_x, at_y):
        return h * 16 + at_x * 4 + at_y

    def primary(h, a):
        return col(zl, plus(x, a * (1 - h)), plus(y, a * h))

    def second(h, q):
        return col(zl, plus(x, q * h), plus(y, q * (1 - h)))

    def to(src, dst, send, recv, row, to_col):
        return pltpu.make_async_remote_copy(
            src_ref=src, dst_ref=dst, send_sem=send, recv_sem=recv,
            device_id={"row": row, "col": to_col}, device_id_type=pl.DeviceIdType.MESH,
        )

    def loads(i):
        part = pl.ds(i * CHUNK, CHUNK)
        return pltpu.make_async_copy(values.at[part], land.at[part], asem.at[i])

    barrier = pltpu.get_barrier_semaphore()
    greeted = [(sib, c), (r, col(1 - zl, x, y))]
    for d in range(1, 4):
        greeted += [(plus(zh, d) * 2 + core, c), (r, primary(0, d)), (r, primary(1, d))]
    for row, at in greeted:
        pl.semaphore_signal(barrier, 1, device_id={"row": row, "col": at}, device_id_type=pl.DeviceIdType.MESH)

    for i in range(CHUNKS):
        loads(i).start()

    lane = lax.broadcasted_iota(jnp.int32, (1, SLOTS), 1)
    position = jnp.where(lane < count[0, 0], rows[...] * COLS + cols[...], -1)
    posbuf[...] = jnp.full((1, WIDE), -1.0, F32)
    posbuf[:, :SLOTS] = position.astype(F32)
    along = jnp.broadcast_to(posbuf[...], (WIDE, WIDE))
    down = along.T[:SLOTS]
    j = lax.broadcasted_iota(jnp.int32, (SLOTS, WIDE), 0)
    k = lax.broadcasted_iota(jnp.int32, (SLOTS, WIDE), 1)
    prev = jnp.max(jnp.where((down == along[:SLOTS]) & (j < k) & (down >= 0.0), j, -1), axis=0, keepdims=True)
    last = jnp.max(jnp.where(down == k.astype(F32), j, -1), axis=0, keepdims=True)
    tabv[0:1, :] = jnp.where(prev < 0, SLOTS, prev)
    tabv[1:2, :] = jnp.where(last < 0, SLOTS, last)
    tables = pltpu.make_async_copy(tabv, tab, tsem)
    tables.start()

    pl.semaphore_wait(barrier, len(greeted))

    def xcopy(src, slot, send, row):
        return to(src, xbuf.at[slot], xs.at[send], xr.at[slot], row, c)

    for d in (2, 1, 3):
        xcopy(feat, r, d, plus(zh, d) * 2 + core).start()
    xcopy(feat, r, 0, sib).start()
    ccopy = to(cot, cotbuf.at[zl], cs, cr, r, col(1 - zl, x, y))
    ccopy.start()
    xbuf[r] = feat[...]
    cotbuf[zl] = cot[...]

    summed[SLOTS] = jnp.zeros((B, B), F32)
    pieces[SLOTS] = jnp.zeros((B, 2 * B), BF16)
    tables.wait()

    def prepare(i):
        loads(i).wait()

        @pl.loop(i * CHUNK, (i + 1) * CHUNK)
        def _(s):
            v = land[s] + summed[tab[0, s]]
            summed[s] = v
            hi, lo = split(v)
            pieces[s, :, :B] = hi
            pieces[s, :, B:] = lo

    def block(at, i):
        return pieces[tab[1, at * COLS + i]]

    for i in range(CHUNKS):
        prepare(i)

    for d in (1, 3, 2):
        slot = plus(zh, 4 - d) * 2 + core
        xcopy(feat, slot, d, sib).wait_recv()
        xcopy(xbuf.at[slot], slot, 3 + d, sib).start()

    for d in range(4):
        slot = plus(zh, d) * 2 + (1 - core)
        xcopy(feat, slot, 0, sib).wait_recv()
    for i in range(COLS):
        hi, lo = split(xbuf[i])
        xx[i, :B, :B] = hi
        xx[i, B:, :B] = hi
        xx[i, :B, B:] = lo
        xx[i, B:, B:] = lo

    def y1copy(h, q, a):
        slot = h * 16 + q * 4 + a
        return to(ysend.at[slot], yrecv.at[slot], ys.at[slot], yr.at[slot], r, primary(h, a))

    @pl.loop(0, 8)
    def _(g):
        h, q = lax.rem(g, 2), plus(lax.div(g, 2), 1)
        at = [col(h, plus(x, a * (1 - h) + q * h), plus(y, q * (1 - h) + a * h)) for a in range(4)]
        acc = jnp.zeros((4 * B, 2 * B), F32)
        for i in range(COLS):
            lhs = jnp.concatenate([block(n, i) for n in at], axis=0)
            acc = acc + jnp.dot(lhs, xx[i], preferred_element_type=F32)
        for a in range(4):
            part = acc[a * B : (a + 1) * B]
            ysend[h * 16 + q * 4 + a] = part[:, :B] + part[:, B:]
        for a in (2, 1, 3):
            y1copy(h, q, a).start()

    def y2copy(h, q):
        slot = h * 4 + q
        return to(y2send.at[slot], y2recv.at[slot], y2s.at[slot], y2r.at[slot], r, second(h, q))

    def summed_first(h, q):
        slot = h * 16 + q * 4
        for a in range(1, 4):
            y1copy(h, q, a).wait_recv()
        return (ysend[slot] + yrecv[slot + 1]) + (yrecv[slot + 2] + yrecv[slot + 3])

    @pl.loop(0, 6)
    def _(g):
        h, q = lax.rem(g, 2), 1 + lax.div(g, 2)
        y2send[h * 4 + q] = summed_first(h, q)
        y2copy(h, q).start()

    def ecopy(h):
        return to(plane.at[h], zplane.at[h], es.at[h], er.at[h], r, col(1 - zl, x, y))

    for h in range(2):
        own = summed_first(h, 0)
        for q in range(1, 4):
            y2copy(h, q).wait_recv()
            own = own + y2recv[h * 4 + q]
        plane[h] = own
        ecopy(h).start()
    ccopy.wait_recv()
    for h in range(2):
        ecopy(h).wait_recv()

    yv = (plane[...] + zplane[...]).reshape(2 * B, B)
    w = weight[...]
    z = jnp.dot(yv, w, precision=HP, preferred_element_type=F32)
    s = jax.nn.sigmoid(z)
    dz = cotbuf[...].reshape(2 * B, B) * (s * (1.0 + z * (1.0 - s)))
    for h in range(2):
        pbuf[h * 16] = lax.dot_general(
            w, dz[h * B : (h + 1) * B], (((1,), (1,)), ((), ())), precision=HP, preferred_element_type=F32
        )

    def pcopy(h, q, a):
        slot = h * 16 + q * 4 + a
        source = slot if q == 0 or a == 0 else h * 16 + a
        where = primary(h, a) if q == 0 else second(h, q)
        if a == 0:
            source = h * 16
        elif q == 0:
            source = h * 16
        return to(pbuf.at[source], pbuf.at[slot], ps.at[slot], pr.at[slot], r, where)

    for a in (1, 3, 2):
        for h in range(2):
            pcopy(h, 0, a).start()
    for q in (1, 3, 2):
        for h in range(2):
            pcopy(h, q, 0).start()

    acts[...] = (z * s).reshape(2, B, B)
    act_out[...] = acts[zl]
    term = lax.dot_general(yv, dz, (((0,), (0,)), ((), ())), precision=HP, preferred_element_type=F32)
    wterm[...] = term.reshape(16, 8, B)

    def wacopy(a):
        there = plus(x, a)
        return to(wterm.at[pl.ds(there * 4, 4)], wa.at[a], was.at[a], war.at[a], r, primary(0, a))

    def wbcopy(a):
        return to(wsum.at[plus(y, a)], wb.at[a], wbs.at[a], wbr.at[a], r, primary(1, a))

    wdcopy = to(wc, wd, wds, wdr, sib, c)

    def wzcopy(a, slot):
        return to(wz.at[slot], wz.at[slot], wzs.at[a], wzr.at[a], plus(zh, a) * 2 + core, c)

    def wycopy(a, at_y):
        return to(wg.at[x, at_y], wg.at[x, at_y], wys.at[a], wyr.at[a], r, primary(1, a))

    def wxcopy(a, at_x):
        return to(wg.at[at_x], wg.at[at_x], wxs.at[a], wxr.at[a], r, primary(0, a))

    for a in range(1, 4):
        wacopy(a).start()
    for i in range(COLS):
        facc[i] = jnp.zeros((B, B), F32)

    for a in (1, 3, 2):
        for h in range(2):
            pcopy(h, 0, a).wait_recv()
            for q in (1, 3, 2):
                pcopy(h, q, a).start()

    def back(g):
        n = lax.div(g, 2)
        h, a = lax.rem(g, 2), lax.rem(lax.div(n * (n + 1), 2), 4)
        base = h * 16 + a
        at = []
        for q in range(4):
            at.append(col(h, plus(x + 8, -(a * (1 - h) + q * h)), plus(y + 8, -(q * (1 - h) + a * h))))
        p = jnp.concatenate([pbuf[base + q * 4] for q in range(4)], axis=1)
        hi, lo = split(p)
        lhs = jnp.concatenate([hi, lo], axis=0)
        for i in range(COLS):
            rhs = jnp.concatenate([block(m, i) for m in at], axis=0)
            res = jnp.dot(lhs, rhs, preferred_element_type=F32)
            facc[i] += (res[:B, :B] + res[B:, B:]) + (res[:B, B:] + res[B:, :B])

    def arrive(g):
        n = lax.div(g, 2)
        h, a = lax.rem(g, 2), lax.rem(lax.div(n * (n + 1), 2), 4)
        for q in range(1, 4):
            slot = h * 16 + q * 4 + a
            to(pbuf.at[slot], pbuf.at[slot], ps.at[slot], pr.at[slot], r, second(h, q)).wait_recv()

    def back_groups(lo, hi):
        @pl.loop(lo, hi)
        def _(g):
            arrive(g)
            back(g)

    back_groups(0, 2)
    for a in range(1, 4):
        wacopy(a).wait_recv()
    wsum[...] = (wterm[pl.ds(x * 4, 4)] + wa[1]) + (wa[2] + wa[3])
    for a in range(1, 4):
        wbcopy(a).start()

    back_groups(2, 4)
    for a in range(1, 4):
        wbcopy(a).wait_recv()
    wc[...] = (wsum[y] + wb[1]) + (wb[2] + wb[3])
    wdcopy.start()

    back_groups(4, 5)
    wdcopy.wait_recv()
    wz[zh] = wc[...] + wd[...]
    for a in range(1, 4):
        wzcopy(a, zh).start()

    back_groups(5, 7)
    for a in range(1, 4):
        wzcopy(a, plus(zh, 4 - a)).wait_recv()
    wg[x, y] = (wz[0] + wz[1]) + (wz[2] + wz[3])
    for a in range(1, 4):
        wycopy(a, y).start()

    back_groups(7, 8)

    def scopy(q):
        return to(facc.at[q * 2 + (1 - core)], srecv.at[q], ss.at[q], sr.at[q], sib, c)

    def zcopy(d):
        return to(zsend.at[d], zrecv.at[d], zs.at[d], zr.at[d], plus(zh, d) * 2 + core, c)

    for d in (2, 1, 3, 0):
        scopy(plus(zh, d)).start()
    for d in (2, 1, 3):
        q = plus(zh, d)
        scopy(q).wait_recv()
        zsend[d] = facc[q * 2 + core] + srecv[q]
        zcopy(d).start()
    scopy(zh).wait_recv()
    total = facc[r] + srecv[zh]

    for a in range(1, 4):
        wycopy(a, plus(y, 4 - a)).wait_recv()
    for a in range(1, 4):
        wxcopy(a, x).start()
    for a in range(1, 4):
        wxcopy(a, plus(x, 4 - a)).wait_recv()
    wgrad_out[...] = wg[...].reshape(B, B)

    ccopy.wait_send()
    wdcopy.wait_send()
    xcopy(feat, r, 0, sib).wait_send()
    for a in range(1, 4):
        xcopy(feat, r, a, sib).wait_send()
        xcopy(feat, r, 3 + a, sib).wait_send()
        wacopy(a).wait_send()
        wbcopy(a).wait_send()
        wzcopy(a, zh).wait_send()
        wycopy(a, y).wait_send()
        wxcopy(a, x).wait_send()
    for h in range(2):
        ecopy(h).wait_send()
        for q in range(4):
            scopy(q).wait_send() if h == 0 else None
            if q:
                y2copy(h, q).wait_send()
            for a in range(4):
                if a:
                    y1copy(h, q, a).wait_send()
                if a or q:
                    pcopy(h, q, a).wait_send()

    for d in (1, 3, 2):
        zcopy(d).wait_recv()
        total = total + zrecv[d]
    fgrad_out[...] = total.T
    for d in range(1, 4):
        zcopy(d).wait_send()


def deliver(a, b, c, a_out, b_out, c_out, sems):
    copies = [pltpu.make_async_copy(s, d, sems.at[i]) for i, (s, d) in enumerate([(a, a_out), (b, b_out), (c, c_out)])]
    for copy in copies:
        copy.start()
    for copy in copies:
        copy.wait()


def local(features, block_values, block_rows, block_cols, live_block_count, weight, cotangent):
    vmem = pl.BlockSpec(memory_space=pltpu.VMEM)
    smem = pl.BlockSpec(memory_space=pltpu.SMEM)
    anywhere = pl.BlockSpec(memory_space=pl.ANY)
    dma = pltpu.SemaphoreType.DMA
    results = [jax.ShapeDtypeStruct((B, B), F32)] * 3

    def blocks(n):
        return pltpu.VMEM((n, B, B), F32)

    outs = pl.pallas_call(
        kernel,
        out_shape=results,
        in_specs=[smem, vmem, vmem, vmem, vmem, vmem, anywhere],
        out_specs=[vmem, vmem, vmem],
        scratch_shapes=[
            blocks(SLOTS),
            blocks(SLOTS + 1),
            pltpu.VMEM((SLOTS + 1, B, 2 * B), BF16),
            pltpu.VMEM((1, WIDE), F32),
            pltpu.VMEM((2, WIDE), jnp.int32),
            pltpu.SMEM((2, WIDE), jnp.int32),
            blocks(COLS),
            pltpu.VMEM((COLS, 2 * B, 2 * B), BF16),
            blocks(2),
            blocks(32),
            blocks(32),
            blocks(8),
            blocks(8),
            blocks(2),
            blocks(2),
            blocks(2),
            blocks(32),
            blocks(COLS),
            blocks(4),
            blocks(4),
            blocks(4),
            pltpu.VMEM((16, 8, B), F32),
            pltpu.VMEM((4, 4, 8, B), F32),
            pltpu.VMEM((4, 8, B), F32),
            pltpu.VMEM((4, 8, B), F32),
            pltpu.VMEM((8, B), F32),
            pltpu.VMEM((8, B), F32),
            pltpu.VMEM((4, 8, B), F32),
            pltpu.VMEM((4, 4, 8, B), F32),
            dma((CHUNKS,)), dma,
            dma((7,)), dma((8,)), dma, dma,
            dma((32,)), dma((32,)), dma((8,)), dma((8,)), dma((2,)), dma((2,)),
            dma((32,)), dma((32,)), dma((4,)), dma((4,)), dma((4,)), dma((4,)),
            dma((4,)), dma((4,)), dma((4,)), dma((4,)), dma, dma,
            dma((4,)), dma((4,)), dma((4,)), dma((4,)), dma((4,)), dma((4,)),
        ],
        compiler_params=pltpu.CompilerParams(
            collective_id=0, has_side_effects=True, vmem_limit_bytes=56 * 1024 * 1024
        ),
    )(
        live_block_count, block_rows[0], block_cols[0], features[0], weight, cotangent[0], block_values[0, 0]
    )
    act, wgrad, fgrad = pl.pallas_call(
        deliver,
        out_shape=results,
        in_specs=[anywhere] * 3,
        out_specs=[anywhere] * 3,
        scratch_shapes=[dma((3,))],
    )(*outs)
    return act[None], wgrad, fgrad[None]


def solution(mesh):
    in_specs = (
        P("col", "row", None),
        P("row", "col", None, None, None),
        P("row", "col", None),
        P("row", "col", None),
        P("row", "col"),
        P(),
        P("row", "col", None),
    )
    out_specs = (P("row", "col", None), P(), P("col", "row", None))
    return jax.shard_map(local, mesh=mesh, in_specs=in_specs, out_specs=out_specs, check_vma=False)
```

```python
import jax
import jax.numpy as jnp
from jax import lax
from jax.experimental import pallas as pl
from jax.experimental.pallas import tpu as pltpu
from jax.sharding import PartitionSpec as P

B = 128
SLOTS = 160
COLS = 8
CHUNK = 20
CHUNKS = SLOTS // CHUNK
WIDE = 256
F32 = jnp.float32
BF16 = jnp.bfloat16
HP = lax.Precision.HIGHEST


def split(v):
    hi = v.astype(BF16)
    return hi, (v - hi.astype(F32)).astype(BF16)


def kernel(
    count, rows, cols, feat, weight, cot, values,
    act_out, wgrad_out, fgrad_out,
    land, summed, pieces, posbuf, tabv, tab, xbuf, xx, cotbuf, ysend, yrecv, y2send, y2recv,
    plane, zplane, acts, pbuf, facc, srecv, zsend, zrecv,
    wterm, wa, wsum, wb, wc, wd, wz, wg,
    asem, tsem, xs, xr, cs, cr, ys, yr, y2s, y2r, es, er, ps, pr, ss, sr, zs, zr,
    was, war, wbs, wbr, wds, wdr, wzs, wzr, wys, wyr, wxs, wxr,
):
    r = lax.axis_index("row")
    c = lax.axis_index("col")
    zh, core = lax.div(r, 2), lax.rem(r, 2)
    zl, x, y = lax.div(c, 16), lax.rem(lax.div(c, 4), 4), lax.rem(c, 4)
    sib = zh * 2 + (1 - core)

    def plus(v, d):
        return lax.rem(v + d, 4)

    def col(h, at_x, at_y):
        return h * 16 + at_x * 4 + at_y

    def primary(h, a):
        return col(zl, plus(x, a * (1 - h)), plus(y, a * h))

    def second(h, q):
        return col(zl, plus(x, q * h), plus(y, q * (1 - h)))

    def to(src, dst, send, recv, row, to_col):
        return pltpu.make_async_remote_copy(
            src_ref=src, dst_ref=dst, send_sem=send, recv_sem=recv,
            device_id={"row": row, "col": to_col}, device_id_type=pl.DeviceIdType.MESH,
        )

    def loads(i):
        part = pl.ds(i * CHUNK, CHUNK)
        return pltpu.make_async_copy(values.at[part], land.at[part], asem.at[i])

    barrier = pltpu.get_barrier_semaphore()
    greeted = [(sib, c), (r, col(1 - zl, x, y))]
    for d in range(1, 4):
        greeted += [(plus(zh, d) * 2 + core, c), (r, primary(0, d)), (r, primary(1, d))]
    for row, at in greeted:
        pl.semaphore_signal(barrier, 1, device_id={"row": row, "col": at}, device_id_type=pl.DeviceIdType.MESH)

    for i in range(CHUNKS):
        loads(i).start()

    pl.semaphore_wait(barrier, len(greeted))

    def xcopy(src, slot, send, row):
        return to(src, xbuf.at[slot], xs.at[send], xr.at[slot], row, c)

    for d in (2, 1, 3):
        xcopy(feat, r, d, plus(zh, d) * 2 + core).start()
    xcopy(feat, r, 0, sib).start()
    ccopy = to(cot, cotbuf.at[zl], cs, cr, r, col(1 - zl, x, y))
    xbuf[r] = feat[...]
    cotbuf[zl] = cot[...]

    lane = lax.broadcasted_iota(jnp.int32, (1, SLOTS), 1)
    position = jnp.where(lane < count[0, 0], rows[...] * COLS + cols[...], -1)
    posbuf[...] = jnp.full((1, WIDE), -1.0, F32)
    posbuf[:, :SLOTS] = position.astype(F32)
    along = jnp.broadcast_to(posbuf[...], (WIDE, WIDE))
    down = along.T[:SLOTS]
    j = lax.broadcasted_iota(jnp.int32, (SLOTS, WIDE), 0)
    k = lax.broadcasted_iota(jnp.int32, (SLOTS, WIDE), 1)
    prev = jnp.max(jnp.where((down == along[:SLOTS]) & (j < k) & (down >= 0.0), j, -1), axis=0, keepdims=True)
    last = jnp.max(jnp.where(down == k.astype(F32), j, -1), axis=0, keepdims=True)
    tabv[0:1, :] = jnp.where(prev < 0, SLOTS, prev)
    tabv[1:2, :] = jnp.where(last < 0, SLOTS, last)
    tables = pltpu.make_async_copy(tabv, tab, tsem)
    tables.start()

    summed[SLOTS] = jnp.zeros((B, B), F32)
    pieces[SLOTS] = jnp.zeros((B, 2 * B), BF16)
    tables.wait()

    def prepare(i):
        loads(i).wait()

        @pl.loop(i * CHUNK, (i + 1) * CHUNK)
        def _(s):
            v = land[s] + summed[tab[0, s]]
            summed[s] = v
            hi, lo = split(v)
            pieces[s, :, :B] = hi
            pieces[s, :, B:] = lo

    def block(at, i):
        return pieces[tab[1, at * COLS + i]]

    for i in range(CHUNKS):
        prepare(i)

    for d in (1, 3, 2):
        slot = plus(zh, 4 - d) * 2 + core
        xcopy(feat, slot, d, sib).wait_recv()
        xcopy(xbuf.at[slot], slot, 3 + d, sib).start()

    for d in range(4):
        slot = plus(zh, d) * 2 + (1 - core)
        xcopy(feat, slot, 0, sib).wait_recv()
    ccopy.start()
    for i in range(COLS):
        hi, lo = split(xbuf[i])
        xx[i, :B, :B] = hi
        xx[i, B:, :B] = hi
        xx[i, :B, B:] = lo
        xx[i, B:, B:] = lo

    def y1copy(h, q, a):
        slot = h * 16 + q * 4 + a
        return to(ysend.at[slot], yrecv.at[slot], ys.at[slot], yr.at[slot], r, primary(h, a))

    @pl.loop(0, 8)
    def _(g):
        h, q = lax.rem(g, 2), plus(lax.div(g, 2), 1)
        at = [col(h, plus(x, a * (1 - h) + q * h), plus(y, q * (1 - h) + a * h)) for a in range(4)]
        acc = jnp.zeros((4 * B, 2 * B), F32)
        for i in range(COLS):
            lhs = jnp.concatenate([block(n, i) for n in at], axis=0)
            acc = acc + jnp.dot(lhs, xx[i], preferred_element_type=F32)
        for a in range(4):
            part = acc[a * B : (a + 1) * B]
            ysend[h * 16 + q * 4 + a] = part[:, :B] + part[:, B:]
        for a in (2, 1, 3):
            y1copy(h, q, a).start()

    def y2copy(h, q):
        slot = h * 4 + q
        return to(y2send.at[slot], y2recv.at[slot], y2s.at[slot], y2r.at[slot], r, second(h, q))

    def summed_first(h, q):
        slot = h * 16 + q * 4
        for a in range(1, 4):
            y1copy(h, q, a).wait_recv()
        return (ysend[slot] + yrecv[slot + 1]) + (yrecv[slot + 2] + yrecv[slot + 3])

    @pl.loop(0, 6)
    def _(g):
        h, q = lax.rem(g, 2), 1 + lax.div(g, 2)
        y2send[h * 4 + q] = summed_first(h, q)
        y2copy(h, q).start()

    def ecopy(h):
        return to(plane.at[h], zplane.at[h], es.at[h], er.at[h], r, col(1 - zl, x, y))

    for h in range(2):
        own = summed_first(h, 0)
        for q in range(1, 4):
            y2copy(h, q).wait_recv()
            own = own + y2recv[h * 4 + q]
        plane[h] = own
        ecopy(h).start()
    ccopy.wait_recv()
    for h in range(2):
        ecopy(h).wait_recv()

    yv = (plane[...] + zplane[...]).reshape(2 * B, B)
    w = weight[...]
    z = jnp.dot(yv, w, precision=HP, preferred_element_type=F32)
    s = jax.nn.sigmoid(z)
    dz = cotbuf[...].reshape(2 * B, B) * (s * (1.0 + z * (1.0 - s)))
    for h in range(2):
        pbuf[h * 16] = lax.dot_general(
            w, dz[h * B : (h + 1) * B], (((1,), (1,)), ((), ())), precision=HP, preferred_element_type=F32
        )

    def pcopy(h, q, a):
        slot = h * 16 + q * 4 + a
        source = slot if q == 0 or a == 0 else h * 16 + a
        where = primary(h, a) if q == 0 else second(h, q)
        if a == 0:
            source = h * 16
        elif q == 0:
            source = h * 16
        return to(pbuf.at[source], pbuf.at[slot], ps.at[slot], pr.at[slot], r, where)

    for a in (1, 3, 2):
        for h in range(2):
            pcopy(h, 0, a).start()

    term = lax.dot_general(yv, dz, (((0,), (0,)), ((), ())), precision=HP, preferred_element_type=F32)
    wterm[...] = term.reshape(16, 8, B)

    def wacopy(a):
        there = plus(x, a)
        return to(wterm.at[pl.ds(there * 4, 4)], wa.at[a], was.at[a], war.at[a], r, primary(0, a))

    def wbcopy(a):
        return to(wsum.at[plus(y, a)], wb.at[a], wbs.at[a], wbr.at[a], r, primary(1, a))

    wdcopy = to(wc, wd, wds, wdr, sib, c)

    def wzcopy(a, slot):
        return to(wz.at[slot], wz.at[slot], wzs.at[a], wzr.at[a], plus(zh, a) * 2 + core, c)

    def wycopy(a, at_y):
        return to(wg.at[x, at_y], wg.at[x, at_y], wys.at[a], wyr.at[a], r, primary(1, a))

    def wxcopy(a, at_x):
        return to(wg.at[at_x], wg.at[at_x], wxs.at[a], wxr.at[a], r, primary(0, a))

    for a in range(1, 4):
        wacopy(a).start()
    for q in (1, 3, 2):
        for h in range(2):
            pcopy(h, q, 0).start()
    acts[...] = (z * s).reshape(2, B, B)
    act_out[...] = acts[zl]
    for i in range(COLS):
        facc[i] = jnp.zeros((B, B), F32)

    for a in (1, 3, 2):
        for h in range(2):
            pcopy(h, 0, a).wait_recv()
            for q in (1, 3, 2):
                pcopy(h, q, a).start()
        if a == 3:
            for d in range(1, 4):
                wacopy(d).wait_recv()
            wsum[...] = (wterm[pl.ds(x * 4, 4)] + wa[1]) + (wa[2] + wa[3])
            for d in range(1, 4):
                wbcopy(d).start()

    def back(g, final=False):
        n = lax.div(g, 2)
        h, a = lax.rem(g, 2), lax.rem(lax.div(n * (n + 1), 2), 4)
        base = h * 16 + a
        at = []
        for q in range(4):
            at.append(col(h, plus(x + 8, -(a * (1 - h) + q * h)), plus(y + 8, -(q * (1 - h) + a * h))))
        p = jnp.concatenate([pbuf[base + q * 4] for q in range(4)], axis=1)
        hi, lo = split(p)
        lhs = jnp.concatenate([hi, lo], axis=0)
        for d in (2, 1, 3, 0):
            row = plus(zh, d)
            for e in range(2):
                i = row * 2 + e
                rhs = jnp.concatenate([block(m, i) for m in at], axis=0)
                res = jnp.dot(lhs, rhs, preferred_element_type=F32)
                facc[i] += (res[:B, :B] + res[B:, B:]) + (res[:B, B:] + res[B:, :B])
            if final:
                scopy(row).start()

    def arrive(g):
        n = lax.div(g, 2)
        h, a = lax.rem(g, 2), lax.rem(lax.div(n * (n + 1), 2), 4)
        for q in range(1, 4):
            slot = h * 16 + q * 4 + a
            to(pbuf.at[slot], pbuf.at[slot], ps.at[slot], pr.at[slot], r, second(h, q)).wait_recv()

    def back_groups(lo, hi):
        @pl.loop(lo, hi)
        def _(g):
            arrive(g)
            back(g)

    def scopy(q):
        return to(facc.at[q * 2 + (1 - core)], srecv.at[q], ss.at[q], sr.at[q], sib, c)

    def zcopy(d):
        return to(zsend.at[d], zrecv.at[d], zs.at[d], zr.at[d], plus(zh, d) * 2 + core, c)

    back_groups(0, 4)
    for a in range(1, 4):
        wbcopy(a).wait_recv()
    wc[...] = (wsum[y] + wb[1]) + (wb[2] + wb[3])
    wdcopy.start()

    back_groups(4, 5)
    wdcopy.wait_recv()
    wz[zh] = wc[...] + wd[...]
    for a in range(1, 4):
        wzcopy(a, zh).start()

    back_groups(5, 7)
    arrive(7)
    back(7, True)

    for d in (2, 1, 3):
        q = plus(zh, d)
        scopy(q).wait_recv()
        zsend[d] = facc[q * 2 + core] + srecv[q]
        zcopy(d).start()
    scopy(zh).wait_recv()
    total = facc[r] + srecv[zh]

    for a in range(1, 4):
        wzcopy(a, plus(zh, 4 - a)).wait_recv()
    wg[x, y] = (wz[0] + wz[1]) + (wz[2] + wz[3])
    for a in range(1, 4):
        wycopy(a, y).start()

    for a in range(1, 4):
        wycopy(a, plus(y, 4 - a)).wait_recv()
    for a in range(1, 4):
        wxcopy(a, x).start()
    for a in range(1, 4):
        wxcopy(a, plus(x, 4 - a)).wait_recv()
    wgrad_out[...] = wg[...].reshape(B, B)

    ccopy.wait_send()
    wdcopy.wait_send()
    xcopy(feat, r, 0, sib).wait_send()
    for a in range(1, 4):
        xcopy(feat, r, a, sib).wait_send()
        xcopy(feat, r, 3 + a, sib).wait_send()
        wacopy(a).wait_send()
        wbcopy(a).wait_send()
        wzcopy(a, zh).wait_send()
        wycopy(a, y).wait_send()
        wxcopy(a, x).wait_send()
    for h in range(2):
        ecopy(h).wait_send()
        for q in range(4):
            scopy(q).wait_send() if h == 0 else None
            if q:
                y2copy(h, q).wait_send()
            for a in range(4):
                if a:
                    y1copy(h, q, a).wait_send()
                if a or q:
                    pcopy(h, q, a).wait_send()

    for d in (1, 3, 2):
        zcopy(d).wait_recv()
        total = total + zrecv[d]
    fgrad_out[...] = total.T
    for d in range(1, 4):
        zcopy(d).wait_send()


def deliver(a, b, c, a_out, b_out, c_out):
    a_out[...] = a[...]
    b_out[...] = b[...]
    c_out[...] = c[...]


def local(features, block_values, block_rows, block_cols, live_block_count, weight, cotangent):
    vmem = pl.BlockSpec(memory_space=pltpu.VMEM)
    smem = pl.BlockSpec(memory_space=pltpu.SMEM)
    anywhere = pl.BlockSpec(memory_space=pl.ANY)
    dma = pltpu.SemaphoreType.DMA
    results = [jax.ShapeDtypeStruct((B, B), F32)] * 3

    def blocks(n):
        return pltpu.VMEM((n, B, B), F32)

    outs = pl.pallas_call(
        kernel,
        out_shape=results,
        in_specs=[smem, vmem, vmem, vmem, vmem, vmem, anywhere],
        out_specs=[vmem, vmem, vmem],
        scratch_shapes=[
            blocks(SLOTS),
            blocks(SLOTS + 1),
            pltpu.VMEM((SLOTS + 1, B, 2 * B), BF16),
            pltpu.VMEM((1, WIDE), F32),
            pltpu.VMEM((2, WIDE), jnp.int32),
            pltpu.SMEM((2, WIDE), jnp.int32),
            blocks(COLS),
            pltpu.VMEM((COLS, 2 * B, 2 * B), BF16),
            blocks(2),
            blocks(32),
            blocks(32),
            blocks(8),
            blocks(8),
            blocks(2),
            blocks(2),
            blocks(2),
            blocks(32),
            blocks(COLS),
            blocks(4),
            blocks(4),
            blocks(4),
            pltpu.VMEM((16, 8, B), F32),
            pltpu.VMEM((4, 4, 8, B), F32),
            pltpu.VMEM((4, 8, B), F32),
            pltpu.VMEM((4, 8, B), F32),
            pltpu.VMEM((8, B), F32),
            pltpu.VMEM((8, B), F32),
            pltpu.VMEM((4, 8, B), F32),
            pltpu.VMEM((4, 4, 8, B), F32),
            dma((CHUNKS,)), dma,
            dma((7,)), dma((8,)), dma, dma,
            dma((32,)), dma((32,)), dma((8,)), dma((8,)), dma((2,)), dma((2,)),
            dma((32,)), dma((32,)), dma((4,)), dma((4,)), dma((4,)), dma((4,)),
            dma((4,)), dma((4,)), dma((4,)), dma((4,)), dma, dma,
            dma((4,)), dma((4,)), dma((4,)), dma((4,)), dma((4,)), dma((4,)),
        ],
        compiler_params=pltpu.CompilerParams(
            collective_id=0, has_side_effects=True, vmem_limit_bytes=56 * 1024 * 1024
        ),
    )(
        live_block_count, block_rows[0], block_cols[0], features[0], weight, cotangent[0], block_values[0, 0]
    )
    act, wgrad, fgrad = pl.pallas_call(
        deliver,
        out_shape=results,
        in_specs=[vmem] * 3,
        out_specs=[vmem] * 3,

    )(*outs)
    return act[None], wgrad, fgrad[None]


def solution(mesh):
    in_specs = (
        P("col", "row", None),
        P("row", "col", None, None, None),
        P("row", "col", None),
        P("row", "col", None),
        P("row", "col"),
        P(),
        P("row", "col", None),
    )
    out_specs = (P("row", "col", None), P(), P("col", "row", None))
    return jax.shard_map(local, mesh=mesh, in_specs=in_specs, out_specs=out_specs, check_vma=False)
```

```python
import jax
import jax.numpy as jnp
from jax import lax
from jax.experimental import pallas as pl
from jax.experimental.pallas import tpu as pltpu
from jax.sharding import PartitionSpec as P

B = 128
SLOTS = 160
COLS = 8
CHUNK = 20
CHUNKS = SLOTS // CHUNK
WIDE = 256
F32 = jnp.float32
BF16 = jnp.bfloat16
HP = lax.Precision.HIGHEST


H = B // 2


def split(v):
    hi = v.astype(BF16)
    return hi, (v - hi.astype(F32)).astype(BF16)


def kernel(
    count, rows, cols, feat, weight, cot, values,
    act_out, wgrad_out, fgrad_out,
    land, summed, pieces, posbuf, tabv, tab, xbuf, xx, cotbuf, ysend, yrecv, y2send, y2recv,
    plane, zplane, acts, pbuf, facc, srecv, zsend, zrecv,
    wterm, wa, wsum, wb, wc, wd, wz, wg,
    asem, tsem, xs, xr, cs, cr, ys, yr, y2s, y2r, es, er, ps, pr, ss, sr, zs, zr,
    was, war, wbs, wbr, wds, wdr, wzs, wzr, wys, wyr, wxs, wxr,
):
    r = lax.axis_index("row")
    c = lax.axis_index("col")
    zh, core = lax.div(r, 2), lax.rem(r, 2)
    zl, x, y = lax.div(c, 16), lax.rem(lax.div(c, 4), 4), lax.rem(c, 4)
    sib = zh * 2 + (1 - core)

    def plus(v, d):
        return lax.rem(v + d, 4)

    def col(h, at_x, at_y):
        return h * 16 + at_x * 4 + at_y

    def primary(h, a):
        return col(zl, plus(x, a * (1 - h)), plus(y, a * h))

    def second(h, q):
        return col(zl, plus(x, q * h), plus(y, q * (1 - h)))

    def to(src, dst, send, recv, row, to_col):
        return pltpu.make_async_remote_copy(
            src_ref=src, dst_ref=dst, send_sem=send, recv_sem=recv,
            device_id={"row": row, "col": to_col}, device_id_type=pl.DeviceIdType.MESH,
        )

    def loads(i):
        part = pl.ds(i * CHUNK, CHUNK)
        return pltpu.make_async_copy(values.at[part], land.at[part], asem.at[i])

    barrier = pltpu.get_barrier_semaphore()
    greeted = [(sib, c), (r, col(1 - zl, x, y))]
    for d in range(1, 4):
        greeted += [(plus(zh, d) * 2 + core, c), (r, primary(0, d)), (r, primary(1, d))]
    for row, at in greeted:
        pl.semaphore_signal(barrier, 1, device_id={"row": row, "col": at}, device_id_type=pl.DeviceIdType.MESH)

    for i in range(CHUNKS):
        loads(i).start()

    pl.semaphore_wait(barrier, len(greeted))

    def xcopy(src, slot, send, row):
        return to(src, xbuf.at[slot], xs.at[send], xr.at[slot], row, c)

    for d in (2, 1, 3):
        xcopy(feat, r, d, plus(zh, d) * 2 + core).start()
    xcopy(feat, r, 0, sib).start()
    ccopy = to(cot, cotbuf.at[zl], cs, cr, r, col(1 - zl, x, y))
    xbuf[r] = feat[...]
    cotbuf[zl] = cot[...]

    lane = lax.broadcasted_iota(jnp.int32, (1, SLOTS), 1)
    position = jnp.where(lane < count[0, 0], rows[...] * COLS + cols[...], -1)
    posbuf[...] = jnp.full((1, WIDE), -1.0, F32)
    posbuf[:, :SLOTS] = position.astype(F32)
    along = jnp.broadcast_to(posbuf[...], (WIDE, WIDE))
    down = along.T[:SLOTS]
    j = lax.broadcasted_iota(jnp.int32, (SLOTS, WIDE), 0)
    k = lax.broadcasted_iota(jnp.int32, (SLOTS, WIDE), 1)
    prev = jnp.max(jnp.where((down == along[:SLOTS]) & (j < k) & (down >= 0.0), j, -1), axis=0, keepdims=True)
    last = jnp.max(jnp.where(down == k.astype(F32), j, -1), axis=0, keepdims=True)
    tabv[0:1, :] = jnp.where(prev < 0, SLOTS, prev)
    tabv[1:2, :] = jnp.where(last < 0, SLOTS, last)
    tables = pltpu.make_async_copy(tabv, tab, tsem)
    tables.start()

    summed[SLOTS] = jnp.zeros((B, B), F32)
    pieces[SLOTS] = jnp.zeros((B, 2 * B), BF16)
    tables.wait()

    def prepare(i):
        loads(i).wait()

        @pl.loop(i * CHUNK, (i + 1) * CHUNK)
        def _(s):
            v = land[s] + summed[tab[0, s]]
            summed[s] = v
            hi, lo = split(v)
            pieces[s, :, :B] = hi
            pieces[s, :, B:] = lo

    def block(at, i):
        return pieces[tab[1, at * COLS + i]]

    for i in range(CHUNKS):
        prepare(i)

    def spread(i):
        hi, lo = split(xbuf[i])
        xx[i, :B, :B] = hi
        xx[i, B:, :B] = hi
        xx[i, :B, B:] = lo
        xx[i, B:, B:] = lo

    xcopy(feat, sib, 0, sib).wait_recv()
    spread(r)
    spread(sib)
    for d in (1, 3, 2):
        slot = plus(zh, 4 - d) * 2 + core
        xcopy(feat, slot, d, sib).wait_recv()
        xcopy(xbuf.at[slot], slot, 3 + d, sib).start()
        spread(slot)

    for d in (1, 3, 2):
        slot = plus(zh, 4 - d) * 2 + (1 - core)
        xcopy(feat, slot, 0, sib).wait_recv()
        spread(slot)
    ccopy.start()

    def at_offset(h, dx, dy):
        return col(h, plus(x, dx), plus(y, dy))

    def half(route):
        return pl.ds(pl.multiple_of(route * H, H), H)

    def y1copy(h, route, a, p):
        n = (h * 2 + route) * 4 + a
        part = pl.ds(2 * p, 2)
        sem = n * 2 + p
        return to(ysend.at[n, part], yrecv.at[n, part], ys.at[sem], yr.at[sem], r, primary(route, a))

    def unit(h, route, p):
        at = []
        for a in range(4):
            for e in range(2):
                q = plus(2 * p + e, 1)
                at.append(at_offset(h, a * (1 - route) + q * route, q * (1 - route) + a * route))
        acc = jnp.zeros((8 * H, 2 * B), F32)
        for i in range(COLS):
            lhs = jnp.concatenate([pieces[tab[1, n * COLS + i], half(route)] for n in at], axis=0)
            acc = acc + jnp.dot(lhs, xx[i], preferred_element_type=F32)
        for a in range(4):
            for e in range(2):
                part = acc[(a * 2 + e) * H : (a * 2 + e + 1) * H]
                ysend[(h * 2 + route) * 4 + a, 2 * p + e] = part[:, :B] + part[:, B:]
        for a in (2, 1, 3):
            y1copy(h, route, a, p).start()

    def units(h, p):
        @pl.loop(0, 2)
        def _(route):
            unit(h, route, p)

    def y2copy(h, route, q):
        n = (h * 2 + route) * 4 + q
        return to(y2send.at[n], y2recv.at[n], y2s.at[n], y2r.at[n], r, second(route, q))

    def y1sum(h, route, place):
        n = (h * 2 + route) * 4
        return (ysend[n, place] + yrecv[n + 1, place]) + (yrecv[n + 2, place] + yrecv[n + 3, place])

    def relay_sums(h, p):
        for route in range(2):
            for a in range(1, 4):
                y1copy(h, route, a, p).wait_recv()
            for q in ((1, 2) if p == 0 else (3,)):
                y2send[(h * 2 + route) * 4 + q] = y1sum(h, route, q - 1)
                y2copy(h, route, q).start()

    def ecopy(h):
        return to(plane.at[h], zplane.at[h], es.at[h], er.at[h], r, col(1 - zl, x, y))

    def exchange(h):
        for route in range(2):
            own = y1sum(h, route, 3)
            for q in range(1, 4):
                y2copy(h, route, q).wait_recv()
                own = own + y2recv[(h * 2 + route) * 4 + q]
            plane[h, route * H : (route + 1) * H] = own
        ecopy(h).start()

    w = weight[...]

    def pcopy(h, route, q, a):
        sem = (h * 2 + route) * 16 + q * 4 + a
        origin = 0 if q == 0 or a == 0 else a
        dx, dy = a * (1 - route) + q * route, q * (1 - route) + a * route
        source = h * 16 + origin * (4 - 3 * route)
        where = primary(route, a) if q == 0 else second(route, q)
        rows = slice(route * H, (route + 1) * H)
        return to(
            pbuf.at[source, rows], pbuf.at[h * 16 + dx * 4 + dy, rows], ps.at[sem], pr.at[sem], r, where
        )

    def middle(h):
        yv = plane[h] + zplane[h]
        z = jnp.dot(yv, w, precision=HP, preferred_element_type=F32)
        s = jax.nn.sigmoid(z)
        dz = cotbuf[h] * (s * (1.0 + z * (1.0 - s)))
        pbuf[h * 16] = lax.dot_general(w, dz, (((1,), (1,)), ((), ())), precision=HP, preferred_element_type=F32)
        for a in (1, 3, 2):
            for route in range(2):
                pcopy(h, route, 0, a).start()
        term = lax.dot_general(yv, dz, (((0,), (0,)), ((), ())), precision=HP, preferred_element_type=F32)
        acts[h] = z * s
        return term.reshape(16, 8, B)

    def direct(h):
        for q in (1, 3, 2):
            for route in range(2):
                pcopy(h, route, q, 0).start()

    def relay(h, a):
        for route in range(2):
            pcopy(h, route, 0, a).wait_recv()
            for q in (1, 3, 2):
                pcopy(h, route, q, a).start()

    def wacopy(a):
        there = plus(x, a)
        return to(wterm.at[pl.ds(there * 4, 4)], wa.at[a], was.at[a], war.at[a], r, primary(0, a))

    def wbcopy(a):
        return to(wsum.at[plus(y, a)], wb.at[a], wbs.at[a], wbr.at[a], r, primary(1, a))

    wdcopy = to(wc, wd, wds, wdr, sib, c)

    def wzcopy(a, slot):
        return to(wz.at[slot], wz.at[slot], wzs.at[a], wzr.at[a], plus(zh, a) * 2 + core, c)

    def wycopy(a, at_y):
        return to(wg.at[x, at_y], wg.at[x, at_y], wys.at[a], wyr.at[a], r, primary(1, a))

    def wxcopy(a, at_x):
        return to(wg.at[at_x], wg.at[at_x], wxs.at[a], wxr.at[a], r, primary(0, a))

    def scopy(q):
        return to(facc.at[q * 2 + (1 - core)], srecv.at[q], ss.at[q], sr.at[q], sib, c)

    def zcopy(d):
        return to(zsend.at[d], zrecv.at[d], zs.at[d], zr.at[d], plus(zh, d) * 2 + core, c)

    def back(h, route, a, final=False):
        at, ps_t = [], []
        for q in range(4):
            dx, dy = a * (1 - route) + q * route, q * (1 - route) + a * route
            at.append(col(h, plus(x + 4, -dx), plus(y + 4, -dy)))
            ps_t.append(pbuf[h * 16 + dx * 4 + dy, half(route)])
        hi, lo = split(jnp.concatenate(ps_t, axis=1))
        lhs = jnp.concatenate([hi, lo], axis=0)
        for d in (2, 1, 3, 0):
            row = plus(zh, d)
            for e in range(2):
                i = row * 2 + e
                rhs = jnp.concatenate([block(m, i) for m in at], axis=0)
                res = jnp.dot(lhs, rhs, preferred_element_type=F32)
                facc[i, half(route)] += (res[:H, :B] + res[H:, B:]) + (res[:H, B:] + res[H:, :B])
            if final:
                scopy(row).start()

    def arrive(h, route, a):
        dy = a * route
        for q in range(1, 4):
            sem = (h * 2 + route) * 16 + q * 4 + a
            place = pbuf.at[h * 16 + (a * (1 - route) + q * route) * 4 + q * (1 - route) + dy, half(route)]
            to(place, place, ps.at[sem], pr.at[sem], r, second(route, q)).wait_recv()

    def back_groups(h, lo, hi):
        @pl.loop(lo, hi)
        def _(g):
            n = lax.div(g, 2)
            route, a = lax.rem(g, 2), lax.rem(lax.div(n * (n + 1), 2), 4)
            arrive(h, route, a)
            back(h, route, a)

    units(0, 0)
    units(0, 1)
    units(1, 0)
    relay_sums(0, 0)
    relay_sums(0, 1)
    units(1, 1)
    relay_sums(1, 0)
    exchange(0)
    for i in range(COLS):
        facc[i] = jnp.zeros((B, B), F32)
    relay_sums(1, 1)
    ccopy.wait_recv()
    ecopy(0).wait_recv()
    wterm[...] = middle(0)
    direct(0)
    exchange(1)
    for a in (1, 3, 2):
        relay(0, a)
    ecopy(1).wait_recv()
    wterm[...] += middle(1)
    for a in range(1, 4):
        wacopy(a).start()
    direct(1)
    act_out[...] = acts[zl]

    back_groups(0, 0, 6)
    for a in range(1, 4):
        wacopy(a).wait_recv()
    wsum[...] = (wterm[pl.ds(x * 4, 4)] + wa[1]) + (wa[2] + wa[3])
    for a in range(1, 4):
        wbcopy(a).start()
    for a in (1, 3, 2):
        relay(1, a)
    back_groups(0, 6, 8)
    back_groups(1, 0, 2)
    for a in range(1, 4):
        wbcopy(a).wait_recv()
    wc[...] = (wsum[y] + wb[1]) + (wb[2] + wb[3])
    wdcopy.start()
    back_groups(1, 2, 4)
    wdcopy.wait_recv()
    wz[zh] = wc[...] + wd[...]
    for a in range(1, 4):
        wzcopy(a, zh).start()
    back_groups(1, 4, 7)
    arrive(1, 1, 2)
    back(1, 1, 2, True)

    for d in (2, 1, 3):
        q = plus(zh, d)
        scopy(q).wait_recv()
        zsend[d] = facc[q * 2 + core] + srecv[q]
        zcopy(d).start()
    scopy(zh).wait_recv()
    total = facc[r] + srecv[zh]

    for a in range(1, 4):
        wzcopy(a, plus(zh, 4 - a)).wait_recv()
    wg[x, y] = (wz[0] + wz[1]) + (wz[2] + wz[3])
    for a in range(1, 4):
        wycopy(a, y).start()

    for a in range(1, 4):
        wycopy(a, plus(y, 4 - a)).wait_recv()
    for a in range(1, 4):
        wxcopy(a, x).start()
    for a in range(1, 4):
        wxcopy(a, plus(x, 4 - a)).wait_recv()
    wgrad_out[...] = wg[...].reshape(B, B)

    ccopy.wait_send()
    wdcopy.wait_send()
    xcopy(feat, r, 0, sib).wait_send()
    for a in range(1, 4):
        xcopy(feat, r, a, sib).wait_send()
        xcopy(feat, r, 3 + a, sib).wait_send()
        wacopy(a).wait_send()
        wbcopy(a).wait_send()
        wzcopy(a, zh).wait_send()
        wycopy(a, y).wait_send()
        wxcopy(a, x).wait_send()
    for q in range(4):
        scopy(q).wait_send()
    for h in range(2):
        ecopy(h).wait_send()
        for route in range(2):
            for a in range(1, 4):
                y1copy(h, route, a, 0).wait_send()
                y1copy(h, route, a, 1).wait_send()
                y2copy(h, route, a).wait_send()
            for q in range(4):
                for a in range(4):
                    if a or q:
                        pcopy(h, route, q, a).wait_send()

    for d in (1, 3, 2):
        zcopy(d).wait_recv()
        total = total + zrecv[d]
    fgrad_out[...] = total.T
    for d in range(1, 4):
        zcopy(d).wait_send()


def deliver(a, b, c, a_out, b_out, c_out):
    a_out[...] = a[...]
    b_out[...] = b[...]
    c_out[...] = c[...]


def local(features, block_values, block_rows, block_cols, live_block_count, weight, cotangent):
    vmem = pl.BlockSpec(memory_space=pltpu.VMEM)
    smem = pl.BlockSpec(memory_space=pltpu.SMEM)
    anywhere = pl.BlockSpec(memory_space=pl.ANY)
    dma = pltpu.SemaphoreType.DMA
    results = [jax.ShapeDtypeStruct((B, B), F32)] * 3

    def blocks(n):
        return pltpu.VMEM((n, B, B), F32)

    outs = pl.pallas_call(
        kernel,
        out_shape=results,
        in_specs=[smem, vmem, vmem, vmem, vmem, vmem, anywhere],
        out_specs=[vmem, vmem, vmem],
        scratch_shapes=[
            blocks(SLOTS),
            blocks(SLOTS + 1),
            pltpu.VMEM((SLOTS + 1, B, 2 * B), BF16),
            pltpu.VMEM((1, WIDE), F32),
            pltpu.VMEM((2, WIDE), jnp.int32),
            pltpu.SMEM((2, WIDE), jnp.int32),
            blocks(COLS),
            pltpu.VMEM((COLS, 2 * B, 2 * B), BF16),
            blocks(2),
            pltpu.VMEM((16, 4, H, B), F32),
            pltpu.VMEM((16, 4, H, B), F32),
            pltpu.VMEM((16, H, B), F32),
            pltpu.VMEM((16, H, B), F32),
            blocks(2),
            blocks(2),
            blocks(2),
            blocks(32),
            blocks(COLS),
            blocks(4),
            blocks(4),
            blocks(4),
            pltpu.VMEM((16, 8, B), F32),
            pltpu.VMEM((4, 4, 8, B), F32),
            pltpu.VMEM((4, 8, B), F32),
            pltpu.VMEM((4, 8, B), F32),
            pltpu.VMEM((8, B), F32),
            pltpu.VMEM((8, B), F32),
            pltpu.VMEM((4, 8, B), F32),
            pltpu.VMEM((4, 4, 8, B), F32),
            dma((CHUNKS,)), dma,
            dma((7,)), dma((8,)), dma, dma,
            dma((32,)), dma((32,)), dma((16,)), dma((16,)), dma((2,)), dma((2,)),
            dma((64,)), dma((64,)), dma((4,)), dma((4,)), dma((4,)), dma((4,)),
            dma((4,)), dma((4,)), dma((4,)), dma((4,)), dma, dma,
            dma((4,)), dma((4,)), dma((4,)), dma((4,)), dma((4,)), dma((4,)),
        ],
        compiler_params=pltpu.CompilerParams(
            collective_id=0, has_side_effects=True, vmem_limit_bytes=56 * 1024 * 1024
        ),
    )(
        live_block_count, block_rows[0], block_cols[0], features[0], weight, cotangent[0], block_values[0, 0]
    )
    act, wgrad, fgrad = pl.pallas_call(
        deliver,
        out_shape=results,
        in_specs=[vmem] * 3,
        out_specs=[vmem] * 3,

    )(*outs)
    return act[None], wgrad, fgrad[None]


def solution(mesh):
    in_specs = (
        P("col", "row", None),
        P("row", "col", None, None, None),
        P("row", "col", None),
        P("row", "col", None),
        P("row", "col"),
        P(),
        P("row", "col", None),
    )
    out_specs = (P("row", "col", None), P(), P("col", "row", None))
    return jax.shard_map(local, mesh=mesh, in_specs=in_specs, out_specs=out_specs, check_vma=False)
```

```python
import jax
import jax.numpy as jnp
from jax import lax
from jax.experimental import pallas as pl
from jax.experimental.pallas import tpu as pltpu
from jax.sharding import PartitionSpec as P

B = 128
SLOTS = 160
COLS = 8
CHUNK = 20
CHUNKS = SLOTS // CHUNK
WIDE = 256
F32 = jnp.float32
BF16 = jnp.bfloat16
HP = lax.Precision.HIGHEST


H = B // 2


def split(v):
    hi = v.astype(BF16)
    return hi, (v - hi.astype(F32)).astype(BF16)


def kernel(
    count, rows_in, cols_in, feat, weight_in, cot, values,
    act_out, wgrad_out, fgrad_out,
    rows, cols, weight, land, summed, pieces, posbuf, tabv, tab, xbuf, xx, cotbuf, ysend, yrecv, y2send, y2recv,
    plane, zplane, acts, pbuf, facc, srecv, zsend, zrecv,
    wterm, wa, wsum, wb, wc, wd, wz, wg,
    isem, asem, tsem, xs, xr, cs, cr, ys, yr, y2s, y2r, es, er, ps, pr, ss, sr, zs, zr,
    was, war, wbs, wbr, wds, wdr, wzs, wzr, wys, wyr, wxs, wxr,
):
    r = lax.axis_index("row")
    c = lax.axis_index("col")
    zh, core = lax.div(r, 2), lax.rem(r, 2)
    zl, x, y = lax.div(c, 16), lax.rem(lax.div(c, 4), 4), lax.rem(c, 4)
    sib = zh * 2 + (1 - core)

    def plus(v, d):
        return lax.rem(v + d, 4)

    def col(h, at_x, at_y):
        return h * 16 + at_x * 4 + at_y

    def primary(h, a):
        return col(zl, plus(x, a * (1 - h)), plus(y, a * h))

    def second(h, q):
        return col(zl, plus(x, q * h), plus(y, q * (1 - h)))

    def to(src, dst, send, recv, row, to_col):
        return pltpu.make_async_remote_copy(
            src_ref=src, dst_ref=dst, send_sem=send, recv_sem=recv,
            device_id={"row": row, "col": to_col}, device_id_type=pl.DeviceIdType.MESH,
        )

    def loads(i):
        part = pl.ds(i * CHUNK, CHUNK)
        return pltpu.make_async_copy(values.at[part], land.at[part], asem.at[i])

    barrier = pltpu.get_barrier_semaphore()
    greeted = [(sib, c), (r, col(1 - zl, x, y))]
    for d in range(1, 4):
        greeted += [(plus(zh, d) * 2 + core, c), (r, primary(0, d)), (r, primary(1, d))]
    for row, at in greeted:
        pl.semaphore_signal(barrier, 1, device_id={"row": row, "col": at}, device_id_type=pl.DeviceIdType.MESH)

    inputs = [(feat, xbuf.at[r]), (rows_in, rows), (cols_in, cols), (cot, cotbuf.at[zl]), (weight_in.at[0], weight)]
    fetch = [pltpu.make_async_copy(src, dst, isem.at[i]) for i, (src, dst) in enumerate(inputs)]
    for copy in fetch:
        copy.start()
    for i in range(CHUNKS):
        loads(i).start()

    pl.semaphore_wait(barrier, len(greeted))

    def xcopy(src, slot, send, row):
        return to(src, xbuf.at[slot], xs.at[send], xr.at[slot], row, c)

    fetch[0].wait()
    for d in (2, 1, 3):
        xcopy(xbuf.at[r], r, d, plus(zh, d) * 2 + core).start()
    xcopy(xbuf.at[r], r, 0, sib).start()
    ccopy = to(cotbuf.at[zl], cotbuf.at[zl], cs, cr, r, col(1 - zl, x, y))

    for copy in fetch[1:]:
        copy.wait()
    lane = lax.broadcasted_iota(jnp.int32, (1, SLOTS), 1)
    position = jnp.where(lane < count[0, 0], rows[...] * COLS + cols[...], -1)
    posbuf[...] = jnp.full((1, WIDE), -1.0, F32)
    posbuf[:, :SLOTS] = position.astype(F32)
    along = jnp.broadcast_to(posbuf[...], (WIDE, WIDE))
    down = along.T[:SLOTS]
    j = lax.broadcasted_iota(jnp.int32, (SLOTS, WIDE), 0)
    k = lax.broadcasted_iota(jnp.int32, (SLOTS, WIDE), 1)
    prev = jnp.max(jnp.where((down == along[:SLOTS]) & (j < k) & (down >= 0.0), j, -1), axis=0, keepdims=True)
    last = jnp.max(jnp.where(down == k.astype(F32), j, -1), axis=0, keepdims=True)
    tabv[0:1, :] = jnp.where(prev < 0, SLOTS, prev)
    tabv[1:2, :] = jnp.where(last < 0, SLOTS, last)
    tables = pltpu.make_async_copy(tabv, tab, tsem)
    tables.start()

    summed[SLOTS] = jnp.zeros((B, B), F32)
    pieces[SLOTS] = jnp.zeros((B, 2 * B), BF16)
    tables.wait()

    def prepare(i):
        loads(i).wait()

        @pl.loop(i * CHUNK, (i + 1) * CHUNK)
        def _(s):
            v = land[s] + summed[tab[0, s]]
            summed[s] = v
            hi, lo = split(v)
            pieces[s, :, :B] = hi
            pieces[s, :, B:] = lo

    def block(at, i):
        return pieces[tab[1, at * COLS + i]]

    for i in range(CHUNKS):
        prepare(i)

    def spread(i):
        hi, lo = split(xbuf[i])
        xx[i, :B, :B] = hi
        xx[i, B:, :B] = hi
        xx[i, :B, B:] = lo
        xx[i, B:, B:] = lo

    xcopy(xbuf.at[r], sib, 0, sib).wait_recv()
    spread(r)
    spread(sib)
    for d in (1, 3, 2):
        slot = plus(zh, 4 - d) * 2 + core
        xcopy(xbuf.at[r], slot, d, sib).wait_recv()
        xcopy(xbuf.at[slot], slot, 3 + d, sib).start()
        spread(slot)

    for d in (1, 3, 2):
        slot = plus(zh, 4 - d) * 2 + (1 - core)
        xcopy(xbuf.at[r], slot, 0, sib).wait_recv()
        spread(slot)
    ccopy.start()

    def at_offset(h, dx, dy):
        return col(h, plus(x, dx), plus(y, dy))

    def half(route):
        return pl.ds(pl.multiple_of(route * H, H), H)

    def y1copy(h, route, a, p):
        n = (h * 2 + route) * 4 + a
        part = pl.ds(2 * p, 2)
        sem = n * 2 + p
        return to(ysend.at[n, part], yrecv.at[n, part], ys.at[sem], yr.at[sem], r, primary(route, a))

    def unit(h, route, p):
        at = []
        for a in range(4):
            for e in range(2):
                q = plus(2 * p + e, 1)
                at.append(at_offset(h, a * (1 - route) + q * route, q * (1 - route) + a * route))
        acc = jnp.zeros((8 * H, 2 * B), F32)
        for i in range(COLS):
            lhs = jnp.concatenate([pieces[tab[1, n * COLS + i], half(route)] for n in at], axis=0)
            acc = acc + jnp.dot(lhs, xx[i], preferred_element_type=F32)
        for a in range(4):
            for e in range(2):
                part = acc[(a * 2 + e) * H : (a * 2 + e + 1) * H]
                ysend[(h * 2 + route) * 4 + a, 2 * p + e] = part[:, :B] + part[:, B:]
        for a in (2, 1, 3):
            y1copy(h, route, a, p).start()

    def units(h, p):
        @pl.loop(0, 2)
        def _(route):
            unit(h, route, p)

    def y2copy(h, route, q):
        n = (h * 2 + route) * 4 + q
        return to(y2send.at[n], y2recv.at[n], y2s.at[n], y2r.at[n], r, second(route, q))

    def y1sum(h, route, place):
        n = (h * 2 + route) * 4
        return (ysend[n, place] + yrecv[n + 1, place]) + (yrecv[n + 2, place] + yrecv[n + 3, place])

    def relay_sums(h, p):
        for route in range(2):
            for a in range(1, 4):
                y1copy(h, route, a, p).wait_recv()
            for q in ((1, 2) if p == 0 else (3,)):
                y2send[(h * 2 + route) * 4 + q] = y1sum(h, route, q - 1)
                y2copy(h, route, q).start()

    def ecopy(h, route):
        rows = slice(route * H, (route + 1) * H)
        n = h * 2 + route
        return to(plane.at[h, rows], zplane.at[h, rows], es.at[n], er.at[n], r, col(1 - zl, x, y))

    def exchange(h):
        for route in range(2):
            own = y1sum(h, route, 3)
            for q in range(1, 4):
                y2copy(h, route, q).wait_recv()
                own = own + y2recv[(h * 2 + route) * 4 + q]
            plane[h, route * H : (route + 1) * H] = own
            ecopy(h, route).start()

    w = weight[...]

    def pcopy(h, route, q, a):
        sem = (h * 2 + route) * 16 + q * 4 + a
        origin = 0 if q == 0 or a == 0 else a
        dx, dy = a * (1 - route) + q * route, q * (1 - route) + a * route
        source = h * 16 + origin * (4 - 3 * route)
        where = primary(route, a) if q == 0 else second(route, q)
        rows = slice(route * H, (route + 1) * H)
        return to(
            pbuf.at[source, rows], pbuf.at[h * 16 + dx * 4 + dy, rows], ps.at[sem], pr.at[sem], r, where
        )

    def middle(h):
        yv = plane[h] + zplane[h]
        z = jnp.dot(yv, w, precision=HP, preferred_element_type=F32)
        s = jax.nn.sigmoid(z)
        dz = cotbuf[h] * (s * (1.0 + z * (1.0 - s)))
        pbuf[h * 16] = lax.dot_general(w, dz, (((1,), (1,)), ((), ())), precision=HP, preferred_element_type=F32)
        for a in (1, 3, 2):
            for route in range(2):
                pcopy(h, route, 0, a).start()
        term = lax.dot_general(yv, dz, (((0,), (0,)), ((), ())), precision=HP, preferred_element_type=F32)
        acts[h] = z * s
        return term.reshape(16, 8, B)

    def direct(h):
        for q in (1, 3, 2):
            for route in range(2):
                pcopy(h, route, q, 0).start()

    def relay(h, a):
        for route in range(2):
            pcopy(h, route, 0, a).wait_recv()
            for q in (1, 3, 2):
                pcopy(h, route, q, a).start()

    def wacopy(a):
        there = plus(x, a)
        return to(wterm.at[pl.ds(there * 4, 4)], wa.at[a], was.at[a], war.at[a], r, primary(0, a))

    def wbcopy(a):
        return to(wsum.at[plus(y, a)], wb.at[a], wbs.at[a], wbr.at[a], r, primary(1, a))

    wdcopy = to(wc, wd, wds, wdr, sib, c)

    def wzcopy(a, slot):
        return to(wz.at[slot], wz.at[slot], wzs.at[a], wzr.at[a], plus(zh, a) * 2 + core, c)

    def wycopy(a, at_y):
        return to(wg.at[x, at_y], wg.at[x, at_y], wys.at[a], wyr.at[a], r, primary(1, a))

    def wxcopy(a, at_x):
        return to(wg.at[at_x], wg.at[at_x], wxs.at[a], wxr.at[a], r, primary(0, a))

    def scopy(q):
        return to(facc.at[q * 2 + (1 - core)], srecv.at[q], ss.at[q], sr.at[q], sib, c)

    def zcopy(d):
        return to(zsend.at[d], zrecv.at[d], zs.at[d], zr.at[d], plus(zh, d) * 2 + core, c)

    def back(h, route, a, final=False):
        at, ps_t = [], []
        for q in range(4):
            dx, dy = a * (1 - route) + q * route, q * (1 - route) + a * route
            at.append(col(h, plus(x + 4, -dx), plus(y + 4, -dy)))
            ps_t.append(pbuf[h * 16 + dx * 4 + dy, half(route)])
        hi, lo = split(jnp.concatenate(ps_t, axis=1))
        lhs = jnp.concatenate([hi, lo], axis=0)
        for d in (2, 1, 3, 0):
            row = plus(zh, d)
            for e in range(2):
                i = row * 2 + e
                rhs = jnp.concatenate([block(m, i) for m in at], axis=0)
                res = jnp.dot(lhs, rhs, preferred_element_type=F32)
                facc[i, half(route)] += (res[:H, :B] + res[H:, B:]) + (res[:H, B:] + res[H:, :B])
            if final:
                scopy(row).start()

    def arrive(h, route, a):
        dy = a * route
        for q in range(1, 4):
            sem = (h * 2 + route) * 16 + q * 4 + a
            place = pbuf.at[h * 16 + (a * (1 - route) + q * route) * 4 + q * (1 - route) + dy, half(route)]
            to(place, place, ps.at[sem], pr.at[sem], r, second(route, q)).wait_recv()

    def back_groups(h, lo, hi):
        @pl.loop(lo, hi)
        def _(g):
            n = lax.div(g, 2)
            route, a = lax.rem(g, 2), lax.rem(lax.div(n * (n + 1), 2), 4)
            arrive(h, route, a)
            back(h, route, a)

    units(0, 0)
    units(0, 1)
    units(1, 0)
    relay_sums(0, 0)
    relay_sums(0, 1)
    units(1, 1)
    relay_sums(1, 0)
    exchange(0)
    for i in range(COLS):
        facc[i] = jnp.zeros((B, B), F32)
    relay_sums(1, 1)
    ccopy.wait_recv()
    ecopy(0, 0).wait_recv()
    ecopy(0, 1).wait_recv()
    wterm[...] = middle(0)
    direct(0)
    exchange(1)
    for a in (1, 3, 2):
        relay(0, a)
    ecopy(1, 0).wait_recv()
    ecopy(1, 1).wait_recv()
    wterm[...] += middle(1)
    for a in range(1, 4):
        wacopy(a).start()
    direct(1)
    act_out[...] = acts[zl]

    back_groups(0, 0, 4)
    for a in range(1, 4):
        wacopy(a).wait_recv()
    wsum[...] = (wterm[pl.ds(x * 4, 4)] + wa[1]) + (wa[2] + wa[3])
    for a in range(1, 4):
        wbcopy(a).start()
    back_groups(0, 4, 6)
    for a in (1, 3, 2):
        relay(1, a)
    back_groups(0, 6, 8)
    back_groups(1, 0, 2)
    for a in range(1, 4):
        wbcopy(a).wait_recv()
    wc[...] = (wsum[y] + wb[1]) + (wb[2] + wb[3])
    wdcopy.start()
    back_groups(1, 2, 4)
    wdcopy.wait_recv()
    wz[zh] = wc[...] + wd[...]
    for a in range(1, 4):
        wzcopy(a, zh).start()
    back_groups(1, 4, 7)
    arrive(1, 1, 2)
    back(1, 1, 2, True)

    for d in (2, 1, 3):
        q = plus(zh, d)
        scopy(q).wait_recv()
        zsend[d] = facc[q * 2 + core] + srecv[q]
        zcopy(d).start()
    scopy(zh).wait_recv()
    total = facc[r] + srecv[zh]

    for a in range(1, 4):
        wzcopy(a, plus(zh, 4 - a)).wait_recv()
    wg[x, y] = (wz[0] + wz[1]) + (wz[2] + wz[3])
    for a in range(1, 4):
        wycopy(a, y).start()

    for a in range(1, 4):
        wycopy(a, plus(y, 4 - a)).wait_recv()
    for a in range(1, 4):
        wxcopy(a, x).start()
    for a in range(1, 4):
        wxcopy(a, plus(x, 4 - a)).wait_recv()
    wgrad_out[...] = wg[...].reshape(B, B)

    ccopy.wait_send()
    wdcopy.wait_send()
    xcopy(xbuf.at[r], r, 0, sib).wait_send()
    for a in range(1, 4):
        xcopy(xbuf.at[r], r, a, sib).wait_send()
        xcopy(xbuf.at[r], r, 3 + a, sib).wait_send()
        wacopy(a).wait_send()
        wbcopy(a).wait_send()
        wzcopy(a, zh).wait_send()
        wycopy(a, y).wait_send()
        wxcopy(a, x).wait_send()
    for q in range(4):
        scopy(q).wait_send()
    for h in range(2):
        for route in range(2):
            ecopy(h, route).wait_send()
            for a in range(1, 4):
                y1copy(h, route, a, 0).wait_send()
                y1copy(h, route, a, 1).wait_send()
                y2copy(h, route, a).wait_send()
            for q in range(4):
                for a in range(4):
                    if a or q:
                        pcopy(h, route, q, a).wait_send()

    for d in (1, 3, 2):
        zcopy(d).wait_recv()
        total = total + zrecv[d]
    fgrad_out[...] = total.T
    for d in range(1, 4):
        zcopy(d).wait_send()


def deliver(a, b, c, a_out, b_out, c_out):
    a_out[...] = a[...]
    b_out[...] = b[...]
    c_out[...] = c[...]


def local(features, block_values, block_rows, block_cols, live_block_count, weight, cotangent):
    vmem = pl.BlockSpec(memory_space=pltpu.VMEM)
    anywhere = pl.BlockSpec(memory_space=pl.ANY)
    dma = pltpu.SemaphoreType.DMA
    results = [jax.ShapeDtypeStruct((B, B), F32)] * 3

    def blocks(n):
        return pltpu.VMEM((n, B, B), F32)

    outs = pl.pallas_call(
        kernel,
        out_shape=results,
        in_specs=[pl.BlockSpec(memory_space=pltpu.SMEM)] + [anywhere] * 6,
        out_specs=[vmem, vmem, vmem],
        scratch_shapes=[
            pltpu.VMEM((1, SLOTS), jnp.int32),
            pltpu.VMEM((1, SLOTS), jnp.int32),
            pltpu.VMEM((B, B), F32),
            blocks(SLOTS),
            blocks(SLOTS + 1),
            pltpu.VMEM((SLOTS + 1, B, 2 * B), BF16),
            pltpu.VMEM((1, WIDE), F32),
            pltpu.VMEM((2, WIDE), jnp.int32),
            pltpu.SMEM((2, WIDE), jnp.int32),
            blocks(COLS),
            pltpu.VMEM((COLS, 2 * B, 2 * B), BF16),
            blocks(2),
            pltpu.VMEM((16, 4, H, B), F32),
            pltpu.VMEM((16, 4, H, B), F32),
            pltpu.VMEM((16, H, B), F32),
            pltpu.VMEM((16, H, B), F32),
            blocks(2),
            blocks(2),
            blocks(2),
            blocks(32),
            blocks(COLS),
            blocks(4),
            blocks(4),
            blocks(4),
            pltpu.VMEM((16, 8, B), F32),
            pltpu.VMEM((4, 4, 8, B), F32),
            pltpu.VMEM((4, 8, B), F32),
            pltpu.VMEM((4, 8, B), F32),
            pltpu.VMEM((8, B), F32),
            pltpu.VMEM((8, B), F32),
            pltpu.VMEM((4, 8, B), F32),
            pltpu.VMEM((4, 4, 8, B), F32),
            dma((5,)), dma((CHUNKS,)), dma,
            dma((7,)), dma((8,)), dma, dma,
            dma((32,)), dma((32,)), dma((16,)), dma((16,)), dma((4,)), dma((4,)),
            dma((64,)), dma((64,)), dma((4,)), dma((4,)), dma((4,)), dma((4,)),
            dma((4,)), dma((4,)), dma((4,)), dma((4,)), dma, dma,
            dma((4,)), dma((4,)), dma((4,)), dma((4,)), dma((4,)), dma((4,)),
        ],
        compiler_params=pltpu.CompilerParams(
            collective_id=0, has_side_effects=True, vmem_limit_bytes=56 * 1024 * 1024
        ),
    )(
        live_block_count, block_rows[0], block_cols[0], features[0], weight[None], cotangent[0], block_values[0, 0]
    )
    act, wgrad, fgrad = pl.pallas_call(
        deliver,
        out_shape=results,
        in_specs=[vmem] * 3,
        out_specs=[vmem] * 3,

    )(*outs)
    return act[None], wgrad, fgrad[None]


def solution(mesh):
    in_specs = (
        P("col", "row", None),
        P("row", "col", None, None, None),
        P("row", "col", None),
        P("row", "col", None),
        P("row", "col"),
        P(),
        P("row", "col", None),
    )
    out_specs = (P("row", "col", None), P(), P("col", "row", None))
    return jax.shard_map(local, mesh=mesh, in_specs=in_specs, out_specs=out_specs, check_vma=False)
```

```python
import jax
import jax.numpy as jnp
from jax import lax
from jax.experimental import pallas as pl
from jax.experimental.pallas import tpu as pltpu
from jax.sharding import PartitionSpec as P

B = 128
SLOTS = 160
COLS = 8
CHUNK = 20
CHUNKS = SLOTS // CHUNK
WIDE = 256
F32 = jnp.float32
BF16 = jnp.bfloat16
HP = lax.Precision.HIGHEST


H = B // 2


def split(v):
    hi = v.astype(BF16)
    return hi, (v - hi.astype(F32)).astype(BF16)


def kernel(
    count, rows_in, cols_in, feat, weight_in, cot, values,
    act_out, wgrad_out, fgrad_out,
    rows, cols, weight, land, summed, pieces, posbuf, tabv, tab, xbuf, xx, cotbuf, ysend, yrecv, y2send, y2recv,
    plane, zplane, acts, pbuf, facc, srecv, zsend, zrecv,
    wterm, wa, wsum, wb, wc, wd, wz, wg,
    isem, asem, tsem, xs, xr, cs, cr, ys, yr, y2s, y2r, es, er, ps, pr, ss, sr, zs, zr,
    was, war, wbs, wbr, wds, wdr, wzs, wzr, wys, wyr, wxs, wxr,
):
    r = lax.axis_index("row")
    c = lax.axis_index("col")
    zh, core = lax.div(r, 2), lax.rem(r, 2)
    zl, x, y = lax.div(c, 16), lax.rem(lax.div(c, 4), 4), lax.rem(c, 4)
    sib = zh * 2 + (1 - core)

    def plus(v, d):
        return lax.rem(v + d, 4)

    def col(h, at_x, at_y):
        return h * 16 + at_x * 4 + at_y

    def primary(h, a):
        return col(zl, plus(x, a * (1 - h)), plus(y, a * h))

    def second(h, q):
        return col(zl, plus(x, q * h), plus(y, q * (1 - h)))

    def to(src, dst, send, recv, row, to_col):
        return pltpu.make_async_remote_copy(
            src_ref=src, dst_ref=dst, send_sem=send, recv_sem=recv,
            device_id={"row": row, "col": to_col}, device_id_type=pl.DeviceIdType.MESH,
        )

    def loads(i):
        part = pl.ds(i * CHUNK, CHUNK)
        return pltpu.make_async_copy(values.at[part], land.at[part], asem.at[i])

    barrier = pltpu.get_barrier_semaphore()
    greeted = [(sib, c), (r, col(1 - zl, x, y))]
    for d in range(1, 4):
        greeted += [(plus(zh, d) * 2 + core, c), (r, primary(0, d)), (r, primary(1, d))]
    for row, at in greeted:
        pl.semaphore_signal(barrier, 1, device_id={"row": row, "col": at}, device_id_type=pl.DeviceIdType.MESH)

    inputs = [(feat, xbuf.at[r]), (rows_in, rows), (cols_in, cols), (cot, cotbuf.at[zl]), (weight_in.at[0], weight)]
    fetch = [pltpu.make_async_copy(src, dst, isem.at[i]) for i, (src, dst) in enumerate(inputs)]
    for copy in fetch:
        copy.start()
    for i in range(CHUNKS):
        loads(i).start()

    pl.semaphore_wait(barrier, len(greeted))

    def xcopy(src, slot, send, row):
        return to(src, xbuf.at[slot], xs.at[send], xr.at[slot], row, c)

    fetch[0].wait()
    for d in (2, 1, 3):
        xcopy(xbuf.at[r], r, d, plus(zh, d) * 2 + core).start()
    xcopy(xbuf.at[r], r, 0, sib).start()
    ccopy = to(cotbuf.at[zl], cotbuf.at[zl], cs, cr, r, col(1 - zl, x, y))

    for copy in fetch[1:]:
        copy.wait()
    lane = lax.broadcasted_iota(jnp.int32, (1, SLOTS), 1)
    position = jnp.where(lane < count[0, 0], rows[...] * COLS + cols[...], -1)
    posbuf[...] = jnp.full((1, WIDE), -1.0, F32)
    posbuf[:, :SLOTS] = position.astype(F32)
    along = jnp.broadcast_to(posbuf[...], (WIDE, WIDE))
    down = along.T[:SLOTS]
    j = lax.broadcasted_iota(jnp.int32, (SLOTS, WIDE), 0)
    k = lax.broadcasted_iota(jnp.int32, (SLOTS, WIDE), 1)
    prev = jnp.max(jnp.where((down == along[:SLOTS]) & (j < k) & (down >= 0.0), j, -1), axis=0, keepdims=True)
    last = jnp.max(jnp.where(down == k.astype(F32), j, -1), axis=0, keepdims=True)
    tabv[0:1, :] = jnp.where(prev < 0, SLOTS, prev)
    tabv[1:2, :] = jnp.where(last < 0, SLOTS, last)
    tables = pltpu.make_async_copy(tabv, tab, tsem)
    tables.start()

    summed[SLOTS] = jnp.zeros((B, B), F32)
    pieces[SLOTS] = jnp.zeros((B, 2 * B), BF16)
    tables.wait()

    def prepare(i):
        loads(i).wait()

        @pl.loop(i * CHUNK, (i + 1) * CHUNK)
        def _(s):
            v = land[s] + summed[tab[0, s]]
            summed[s] = v
            hi, lo = split(v)
            pieces[s, :, :B] = hi
            pieces[s, :, B:] = lo

    def block(at, i):
        return pieces[tab[1, at * COLS + i]]

    for i in range(CHUNKS):
        prepare(i)

    def spread(i):
        hi, lo = split(xbuf[i])
        xx[i, :B, :B] = hi
        xx[i, B:, :B] = hi
        xx[i, :B, B:] = lo
        xx[i, B:, B:] = lo

    xcopy(xbuf.at[r], sib, 0, sib).wait_recv()
    spread(r)
    spread(sib)
    for d in (1, 3, 2):
        slot = plus(zh, 4 - d) * 2 + core
        xcopy(xbuf.at[r], slot, d, sib).wait_recv()
        xcopy(xbuf.at[slot], slot, 3 + d, sib).start()
        spread(slot)

    for d in (1, 3, 2):
        slot = plus(zh, 4 - d) * 2 + (1 - core)
        xcopy(xbuf.at[r], slot, 0, sib).wait_recv()
        spread(slot)
    ccopy.start()

    def at_offset(h, dx, dy):
        return col(h, plus(x, dx), plus(y, dy))

    def half(route):
        return pl.ds(pl.multiple_of(route * H, H), H)

    def y1copy(h, route, a, p):
        n = (h * 2 + route) * 4 + a
        part = pl.ds(2 * p, 2)
        sem = n * 2 + p
        return to(ysend.at[n, part], yrecv.at[n, part], ys.at[sem], yr.at[sem], r, primary(route, a))

    def unit(h, route, p):
        at = []
        for a in range(4):
            for e in range(2):
                q = plus(2 * p + e, 1)
                at.append(at_offset(h, a * (1 - route) + q * route, q * (1 - route) + a * route))
        acc = jnp.zeros((8 * H, 2 * B), F32)
        for i in range(COLS):
            lhs = jnp.concatenate([pieces[tab[1, n * COLS + i], half(route)] for n in at], axis=0)
            acc = acc + jnp.dot(lhs, xx[i], preferred_element_type=F32)
        for a in range(4):
            for e in range(2):
                part = acc[(a * 2 + e) * H : (a * 2 + e + 1) * H]
                ysend[(h * 2 + route) * 4 + a, 2 * p + e] = part[:, :B] + part[:, B:]
        for a in (2, 1, 3):
            y1copy(h, route, a, p).start()

    def units(h, p):
        @pl.loop(0, 2)
        def _(route):
            unit(h, route, p)

    def y2copy(h, route, q):
        n = (h * 2 + route) * 4 + q
        return to(y2send.at[n], y2recv.at[n], y2s.at[n], y2r.at[n], r, second(route, q))

    def y1sum(h, route, place):
        n = (h * 2 + route) * 4
        return (ysend[n, place] + yrecv[n + 1, place]) + (yrecv[n + 2, place] + yrecv[n + 3, place])

    def relay_sums(h, p):
        for route in range(2):
            for a in range(1, 4):
                y1copy(h, route, a, p).wait_recv()
            for q in ((1, 2) if p == 0 else (3,)):
                y2send[(h * 2 + route) * 4 + q] = y1sum(h, route, q - 1)
                y2copy(h, route, q).start()

    def ecopy(h, route):
        rows = slice(route * H, (route + 1) * H)
        n = h * 2 + route
        return to(plane.at[h, rows], zplane.at[h, rows], es.at[n], er.at[n], r, col(1 - zl, x, y))

    def exchange(h):
        for route in range(2):
            own = y1sum(h, route, 3)
            for q in range(1, 4):
                y2copy(h, route, q).wait_recv()
                own = own + y2recv[(h * 2 + route) * 4 + q]
            plane[h, route * H : (route + 1) * H] = own
            ecopy(h, route).start()

    w = weight[...]

    def pcopy(h, route, q, a):
        sem = (h * 2 + route) * 16 + q * 4 + a
        origin = 0 if q == 0 or a == 0 else a
        dx, dy = a * (1 - route) + q * route, q * (1 - route) + a * route
        source = h * 16 + origin * (4 - 3 * route)
        where = primary(route, a) if q == 0 else second(route, q)
        rows = slice(route * H, (route + 1) * H)
        return to(
            pbuf.at[source, rows], pbuf.at[h * 16 + dx * 4 + dy, rows], ps.at[sem], pr.at[sem], r, where
        )

    def middle(h):
        yv = plane[h] + zplane[h]
        z = jnp.dot(yv, w, precision=HP, preferred_element_type=F32)
        s = jax.nn.sigmoid(z)
        dz = cotbuf[h] * (s * (1.0 + z * (1.0 - s)))
        pbuf[h * 16] = lax.dot_general(w, dz, (((1,), (1,)), ((), ())), precision=HP, preferred_element_type=F32)
        for a in (1, 3, 2):
            for route in range(2):
                pcopy(h, route, 0, a).start()
        term = lax.dot_general(yv, dz, (((0,), (0,)), ((), ())), precision=HP, preferred_element_type=F32)
        acts[h] = z * s
        return term.reshape(16, 8, B)

    def direct(h):
        for q in (1, 3, 2):
            for route in range(2):
                pcopy(h, route, q, 0).start()

    def relay(h, a):
        for route in range(2):
            pcopy(h, route, 0, a).wait_recv()
            for q in (1, 3, 2):
                pcopy(h, route, q, a).start()

    def wacopy(a):
        there = plus(x, a)
        return to(wterm.at[pl.ds(there * 4, 4)], wa.at[a], was.at[a], war.at[a], r, primary(0, a))

    def wbcopy(a):
        return to(wsum.at[plus(y, a)], wb.at[a], wbs.at[a], wbr.at[a], r, primary(1, a))

    wdcopy = to(wc, wd, wds, wdr, sib, c)

    def wzcopy(a, slot):
        return to(wz.at[slot], wz.at[slot], wzs.at[a], wzr.at[a], plus(zh, a) * 2 + core, c)

    def wycopy(a, at_y):
        return to(wg.at[x, at_y], wg.at[x, at_y], wys.at[a], wyr.at[a], r, primary(1, a))

    def wxcopy(a, at_x):
        return to(wg.at[at_x], wg.at[at_x], wxs.at[a], wxr.at[a], r, primary(0, a))

    def scopy(q):
        return to(facc.at[q * 2 + (1 - core)], srecv.at[q], ss.at[q], sr.at[q], sib, c)

    def zcopy(d):
        return to(zsend.at[d], zrecv.at[d], zs.at[d], zr.at[d], plus(zh, d) * 2 + core, c)

    def back(h, route, a, final=False):
        at, ps_t = [], []
        for q in range(4):
            dx, dy = a * (1 - route) + q * route, q * (1 - route) + a * route
            at.append(col(h, plus(x + 4, -dx), plus(y + 4, -dy)))
            ps_t.append(pbuf[h * 16 + dx * 4 + dy, half(route)])
        hi, lo = split(jnp.concatenate(ps_t, axis=1))
        lhs = jnp.concatenate([hi, lo], axis=0)
        for d in (2, 1, 3, 0):
            row = plus(zh, d)
            for e in range(2):
                i = row * 2 + e
                rhs = jnp.concatenate([block(m, i) for m in at], axis=0)
                res = jnp.dot(lhs, rhs, preferred_element_type=F32)
                facc[i, half(route)] += (res[:H, :B] + res[H:, B:]) + (res[:H, B:] + res[H:, :B])
            if final:
                scopy(row).start()

    def arrive(h, route, a):
        dy = a * route
        for q in range(1, 4):
            sem = (h * 2 + route) * 16 + q * 4 + a
            place = pbuf.at[h * 16 + (a * (1 - route) + q * route) * 4 + q * (1 - route) + dy, half(route)]
            to(place, place, ps.at[sem], pr.at[sem], r, second(route, q)).wait_recv()

    def back_groups(h, lo, hi):
        @pl.loop(lo, hi)
        def _(g):
            n = lax.div(g, 2)
            route, a = lax.rem(g, 2), lax.rem(lax.div(n * (n + 1), 2), 4)
            arrive(h, route, a)
            back(h, route, a)

    units(0, 0)
    units(0, 1)
    units(1, 0)
    relay_sums(0, 0)
    relay_sums(0, 1)
    units(1, 1)
    relay_sums(1, 0)
    exchange(0)
    for i in range(COLS):
        facc[i] = jnp.zeros((B, B), F32)
    relay_sums(1, 1)
    ccopy.wait_recv()
    ecopy(0, 0).wait_recv()
    ecopy(0, 1).wait_recv()
    wterm[...] = middle(0)
    direct(0)
    exchange(1)
    for a in (1, 3, 2):
        relay(0, a)
    ecopy(1, 0).wait_recv()
    ecopy(1, 1).wait_recv()
    wterm[...] += middle(1)
    for a in range(1, 4):
        wacopy(a).start()
    direct(1)
    act_out[...] = acts[zl]

    back_groups(0, 0, 6)
    relay(1, 1)
    for a in range(1, 4):
        wacopy(a).wait_recv()
    wsum[...] = (wterm[pl.ds(x * 4, 4)] + wa[1]) + (wa[2] + wa[3])
    for a in range(1, 4):
        wbcopy(a).start()
    for a in (3, 2):
        relay(1, a)
    back_groups(0, 6, 8)
    back_groups(1, 0, 2)
    for a in range(1, 4):
        wbcopy(a).wait_recv()
    wc[...] = (wsum[y] + wb[1]) + (wb[2] + wb[3])
    wdcopy.start()
    back_groups(1, 2, 4)
    wdcopy.wait_recv()
    wz[zh] = wc[...] + wd[...]
    for a in range(1, 4):
        wzcopy(a, zh).start()
    back_groups(1, 4, 7)
    arrive(1, 1, 2)
    back(1, 1, 2, True)

    for d in (2, 1, 3):
        q = plus(zh, d)
        scopy(q).wait_recv()
        zsend[d] = facc[q * 2 + core] + srecv[q]
        zcopy(d).start()
    scopy(zh).wait_recv()
    total = facc[r] + srecv[zh]

    for a in range(1, 4):
        wzcopy(a, plus(zh, 4 - a)).wait_recv()
    wg[x, y] = (wz[0] + wz[1]) + (wz[2] + wz[3])
    for a in range(1, 4):
        wycopy(a, y).start()

    for a in range(1, 4):
        wycopy(a, plus(y, 4 - a)).wait_recv()
    for a in range(1, 4):
        wxcopy(a, x).start()
    for a in range(1, 4):
        wxcopy(a, plus(x, 4 - a)).wait_recv()
    wgrad_out[...] = wg[...].reshape(B, B)

    ccopy.wait_send()
    wdcopy.wait_send()
    xcopy(xbuf.at[r], r, 0, sib).wait_send()
    for a in range(1, 4):
        xcopy(xbuf.at[r], r, a, sib).wait_send()
        xcopy(xbuf.at[r], r, 3 + a, sib).wait_send()
        wacopy(a).wait_send()
        wbcopy(a).wait_send()
        wzcopy(a, zh).wait_send()
        wycopy(a, y).wait_send()
        wxcopy(a, x).wait_send()
    for q in range(4):
        scopy(q).wait_send()
    for h in range(2):
        for route in range(2):
            ecopy(h, route).wait_send()
            for a in range(1, 4):
                y1copy(h, route, a, 0).wait_send()
                y1copy(h, route, a, 1).wait_send()
                y2copy(h, route, a).wait_send()
            for q in range(4):
                for a in range(4):
                    if a or q:
                        pcopy(h, route, q, a).wait_send()

    for d in (1, 3, 2):
        zcopy(d).wait_recv()
        total = total + zrecv[d]
    fgrad_out[...] = total.T
    for d in range(1, 4):
        zcopy(d).wait_send()


def deliver(a, b, c, a_out, b_out, c_out):
    a_out[...] = a[...]
    b_out[...] = b[...]
    c_out[...] = c[...]


def local(features, block_values, block_rows, block_cols, live_block_count, weight, cotangent):
    vmem = pl.BlockSpec(memory_space=pltpu.VMEM)
    anywhere = pl.BlockSpec(memory_space=pl.ANY)
    dma = pltpu.SemaphoreType.DMA
    results = [jax.ShapeDtypeStruct((B, B), F32)] * 3

    def blocks(n):
        return pltpu.VMEM((n, B, B), F32)

    outs = pl.pallas_call(
        kernel,
        out_shape=results,
        in_specs=[pl.BlockSpec(memory_space=pltpu.SMEM)] + [anywhere] * 6,
        out_specs=[vmem, vmem, vmem],
        scratch_shapes=[
            pltpu.VMEM((1, SLOTS), jnp.int32),
            pltpu.VMEM((1, SLOTS), jnp.int32),
            pltpu.VMEM((B, B), F32),
            blocks(SLOTS),
            blocks(SLOTS + 1),
            pltpu.VMEM((SLOTS + 1, B, 2 * B), BF16),
            pltpu.VMEM((1, WIDE), F32),
            pltpu.VMEM((2, WIDE), jnp.int32),
            pltpu.SMEM((2, WIDE), jnp.int32),
            blocks(COLS),
            pltpu.VMEM((COLS, 2 * B, 2 * B), BF16),
            blocks(2),
            pltpu.VMEM((16, 4, H, B), F32),
            pltpu.VMEM((16, 4, H, B), F32),
            pltpu.VMEM((16, H, B), F32),
            pltpu.VMEM((16, H, B), F32),
            blocks(2),
            blocks(2),
            blocks(2),
            blocks(32),
            blocks(COLS),
            blocks(4),
            blocks(4),
            blocks(4),
            pltpu.VMEM((16, 8, B), F32),
            pltpu.VMEM((4, 4, 8, B), F32),
            pltpu.VMEM((4, 8, B), F32),
            pltpu.VMEM((4, 8, B), F32),
            pltpu.VMEM((8, B), F32),
            pltpu.VMEM((8, B), F32),
            pltpu.VMEM((4, 8, B), F32),
            pltpu.VMEM((4, 4, 8, B), F32),
            dma((5,)), dma((CHUNKS,)), dma,
            dma((7,)), dma((8,)), dma, dma,
            dma((32,)), dma((32,)), dma((16,)), dma((16,)), dma((4,)), dma((4,)),
            dma((64,)), dma((64,)), dma((4,)), dma((4,)), dma((4,)), dma((4,)),
            dma((4,)), dma((4,)), dma((4,)), dma((4,)), dma, dma,
            dma((4,)), dma((4,)), dma((4,)), dma((4,)), dma((4,)), dma((4,)),
        ],
        compiler_params=pltpu.CompilerParams(
            collective_id=0, has_side_effects=True, vmem_limit_bytes=56 * 1024 * 1024
        ),
    )(
        live_block_count, block_rows[0], block_cols[0], features[0], weight[None], cotangent[0], block_values[0, 0]
    )
    act, wgrad, fgrad = pl.pallas_call(
        deliver,
        out_shape=results,
        in_specs=[vmem] * 3,
        out_specs=[vmem] * 3,

    )(*outs)
    return act[None], wgrad, fgrad[None]


def solution(mesh):
    in_specs = (
        P("col", "row", None),
        P("row", "col", None, None, None),
        P("row", "col", None),
        P("row", "col", None),
        P("row", "col"),
        P(),
        P("row", "col", None),
    )
    out_specs = (P("row", "col", None), P(), P("col", "row", None))
    return jax.shard_map(local, mesh=mesh, in_specs=in_specs, out_specs=out_specs, check_vma=False)
```

```python
import jax
import jax.numpy as jnp
from jax import lax
from jax.experimental import pallas as pl
from jax.experimental.pallas import tpu as pltpu
from jax.sharding import PartitionSpec as P

B = 128
SLOTS = 160
COLS = 8
CHUNK = 20
CHUNKS = SLOTS // CHUNK
WIDE = 256
F32 = jnp.float32
BF16 = jnp.bfloat16
HP = lax.Precision.HIGHEST


H = B // 2


def split(v):
    hi = v.astype(BF16)
    return hi, (v - hi.astype(F32)).astype(BF16)


def kernel(
    count, rows_in, cols_in, feat, weight_in, cot, values,
    act_out, wgrad_out, fgrad_out,
    rows, cols, weight, land, summed, pieces, posbuf, tabv, tab, xbuf, xx, cotbuf, ysend, yrecv, y2send, y2recv,
    plane, zplane, acts, pbuf, facc, srecv, zsend, zrecv,
    wterm, wa, wsum, wb, wc, wd, wz, wg,
    isem, asem, tsem, xs, xr, cs, cr, ys, yr, y2s, y2r, es, er, ps, pr, ss, sr, zs, zr,
    was, war, wbs, wbr, wds, wdr, wzs, wzr, wys, wyr, wxs, wxr,
):
    r = lax.axis_index("row")
    c = lax.axis_index("col")
    zh, core = lax.div(r, 2), lax.rem(r, 2)
    zl, x, y = lax.div(c, 16), lax.rem(lax.div(c, 4), 4), lax.rem(c, 4)
    sib = zh * 2 + (1 - core)

    def plus(v, d):
        return lax.rem(v + d, 4)

    def col(h, at_x, at_y):
        return h * 16 + at_x * 4 + at_y

    def primary(h, a):
        return col(zl, plus(x, a * (1 - h)), plus(y, a * h))

    def second(h, q):
        return col(zl, plus(x, q * h), plus(y, q * (1 - h)))

    def to(src, dst, send, recv, row, to_col):
        return pltpu.make_async_remote_copy(
            src_ref=src, dst_ref=dst, send_sem=send, recv_sem=recv,
            device_id={"row": row, "col": to_col}, device_id_type=pl.DeviceIdType.MESH,
        )

    def loads(i):
        part = pl.ds(i * CHUNK, CHUNK)
        return pltpu.make_async_copy(values.at[part], land.at[part], asem.at[i])

    barrier = pltpu.get_barrier_semaphore()
    greeted = [(sib, c), (r, col(1 - zl, x, y))]
    for d in range(1, 4):
        greeted += [(plus(zh, d) * 2 + core, c), (r, primary(0, d)), (r, primary(1, d))]
    for row, at in greeted:
        pl.semaphore_signal(barrier, 1, device_id={"row": row, "col": at}, device_id_type=pl.DeviceIdType.MESH)

    inputs = [(feat, xbuf.at[r]), (rows_in, rows), (cols_in, cols), (cot, cotbuf.at[zl]), (weight_in.at[0], weight)]
    fetch = [pltpu.make_async_copy(src, dst, isem.at[i]) for i, (src, dst) in enumerate(inputs)]
    for copy in fetch:
        copy.start()
    for i in range(CHUNKS):
        loads(i).start()

    pl.semaphore_wait(barrier, len(greeted))

    def xcopy(src, slot, send, row):
        return to(src, xbuf.at[slot], xs.at[send], xr.at[slot], row, c)

    fetch[0].wait()
    for d in (2, 1, 3):
        xcopy(xbuf.at[r], r, d, plus(zh, d) * 2 + core).start()
    xcopy(xbuf.at[r], r, 0, sib).start()
    ccopy = to(cotbuf.at[zl], cotbuf.at[zl], cs, cr, r, col(1 - zl, x, y))

    for copy in fetch[1:]:
        copy.wait()
    lane = lax.broadcasted_iota(jnp.int32, (1, SLOTS), 1)
    position = jnp.where(lane < count[0, 0], rows[...] * COLS + cols[...], -1)
    posbuf[...] = jnp.full((1, WIDE), -1.0, F32)
    posbuf[:, :SLOTS] = position.astype(F32)
    along = jnp.broadcast_to(posbuf[...], (WIDE, WIDE))
    down = along.T[:SLOTS]
    j = lax.broadcasted_iota(jnp.int32, (SLOTS, WIDE), 0)
    k = lax.broadcasted_iota(jnp.int32, (SLOTS, WIDE), 1)
    prev = jnp.max(jnp.where((down == along[:SLOTS]) & (j < k) & (down >= 0.0), j, -1), axis=0, keepdims=True)
    last = jnp.max(jnp.where(down == k.astype(F32), j, -1), axis=0, keepdims=True)
    tabv[0:1, :] = jnp.where(prev < 0, SLOTS, prev)
    tabv[1:2, :] = jnp.where(last < 0, SLOTS, last)
    tables = pltpu.make_async_copy(tabv, tab, tsem)
    tables.start()

    summed[SLOTS] = jnp.zeros((B, B), F32)
    pieces[SLOTS] = jnp.zeros((B, 2 * B), BF16)
    tables.wait()

    def prepare(i):
        loads(i).wait()

        @pl.loop(i * CHUNK, (i + 1) * CHUNK)
        def _(s):
            v = land[s] + summed[tab[0, s]]
            summed[s] = v
            hi, lo = split(v)
            pieces[s, :, :B] = hi
            pieces[s, :, B:] = lo

    def block(at, i):
        return pieces[tab[1, at * COLS + i]]

    for i in range(CHUNKS):
        prepare(i)

    def spread(i):
        hi, lo = split(xbuf[i])
        xx[i, :B, :B] = hi
        xx[i, B:, :B] = hi
        xx[i, :B, B:] = lo
        xx[i, B:, B:] = lo

    xcopy(xbuf.at[r], sib, 0, sib).wait_recv()
    spread(r)
    spread(sib)
    for d in (1, 3, 2):
        slot = plus(zh, 4 - d) * 2 + core
        xcopy(xbuf.at[r], slot, d, sib).wait_recv()
        xcopy(xbuf.at[slot], slot, 3 + d, sib).start()
        spread(slot)

    for d in (1, 3, 2):
        slot = plus(zh, 4 - d) * 2 + (1 - core)
        xcopy(xbuf.at[r], slot, 0, sib).wait_recv()
        spread(slot)
    ccopy.start()

    def at_offset(h, dx, dy):
        return col(h, plus(x, dx), plus(y, dy))

    def half(route):
        return pl.ds(pl.multiple_of(route * H, H), H)

    def y1copy(h, route, a, p):
        n = (h * 2 + route) * 4 + a
        part = pl.ds(2 * p, 2)
        sem = n * 2 + p
        return to(ysend.at[n, part], yrecv.at[n, part], ys.at[sem], yr.at[sem], r, primary(route, a))

    def unit(h, route, p):
        at = []
        for a in range(4):
            for e in range(2):
                q = plus(2 * p + e, 1)
                at.append(at_offset(h, a * (1 - route) + q * route, q * (1 - route) + a * route))
        acc = jnp.zeros((8 * H, 2 * B), F32)
        for i in range(COLS):
            lhs = jnp.concatenate([pieces[tab[1, n * COLS + i], half(route)] for n in at], axis=0)
            acc = acc + jnp.dot(lhs, xx[i], preferred_element_type=F32)
        for a in range(4):
            for e in range(2):
                part = acc[(a * 2 + e) * H : (a * 2 + e + 1) * H]
                ysend[(h * 2 + route) * 4 + a, 2 * p + e] = part[:, :B] + part[:, B:]
        for a in (2, 1, 3):
            y1copy(h, route, a, p).start()

    def units(h, p):
        @pl.loop(0, 2)
        def _(route):
            unit(h, route, p)

    def y2copy(h, route, q):
        n = (h * 2 + route) * 4 + q
        return to(y2send.at[n], y2recv.at[n], y2s.at[n], y2r.at[n], r, second(route, q))

    def y1sum(h, route, place):
        n = (h * 2 + route) * 4
        return (ysend[n, place] + yrecv[n + 1, place]) + (yrecv[n + 2, place] + yrecv[n + 3, place])

    def relay_sums(h, p):
        for route in range(2):
            for a in range(1, 4):
                y1copy(h, route, a, p).wait_recv()
            for q in ((1, 2) if p == 0 else (3,)):
                y2send[(h * 2 + route) * 4 + q] = y1sum(h, route, q - 1)
                y2copy(h, route, q).start()

    def ecopy(h, route):
        rows = slice(route * H, (route + 1) * H)
        n = h * 2 + route
        return to(plane.at[h, rows], zplane.at[h, rows], es.at[n], er.at[n], r, col(1 - zl, x, y))

    def exchange(h):
        for route in range(2):
            own = y1sum(h, route, 3)
            for q in range(1, 4):
                y2copy(h, route, q).wait_recv()
                own = own + y2recv[(h * 2 + route) * 4 + q]
            plane[h, route * H : (route + 1) * H] = own
            ecopy(h, route).start()

    w = weight[...]

    def pcopy(h, route, q, a):
        sem = (h * 2 + route) * 16 + q * 4 + a
        origin = 0 if q == 0 or a == 0 else a
        dx, dy = a * (1 - route) + q * route, q * (1 - route) + a * route
        source = h * 16 + origin * (4 - 3 * route)
        where = primary(route, a) if q == 0 else second(route, q)
        rows = slice(route * H, (route + 1) * H)
        return to(
            pbuf.at[source, rows], pbuf.at[h * 16 + dx * 4 + dy, rows], ps.at[sem], pr.at[sem], r, where
        )

    def middle(h):
        yv = plane[h] + zplane[h]
        z = jnp.dot(yv, w, precision=HP, preferred_element_type=F32)
        s = jax.nn.sigmoid(z)
        dz = cotbuf[h] * (s * (1.0 + z * (1.0 - s)))
        pbuf[h * 16] = lax.dot_general(w, dz, (((1,), (1,)), ((), ())), precision=HP, preferred_element_type=F32)
        for a in (1, 3, 2):
            for route in range(2):
                pcopy(h, route, 0, a).start()
        term = lax.dot_general(yv, dz, (((0,), (0,)), ((), ())), precision=HP, preferred_element_type=F32)
        acts[h] = z * s
        return term.reshape(16, 8, B)

    def direct(h):
        for q in (1, 3, 2):
            for route in range(2):
                pcopy(h, route, q, 0).start()

    def relay(h, a):
        for route in range(2):
            pcopy(h, route, 0, a).wait_recv()
            for q in (1, 3, 2):
                pcopy(h, route, q, a).start()

    def wacopy(a):
        there = plus(x, a)
        return to(wterm.at[pl.ds(there * 4, 4)], wa.at[a], was.at[a], war.at[a], r, primary(0, a))

    def wbcopy(a):
        return to(wsum.at[plus(y, a)], wb.at[a], wbs.at[a], wbr.at[a], r, primary(1, a))

    wdcopy = to(wc, wd, wds, wdr, sib, c)

    def wzcopy(a, slot):
        return to(wz.at[slot], wz.at[slot], wzs.at[a], wzr.at[a], plus(zh, a) * 2 + core, c)

    def wycopy(a, at_y):
        return to(wg.at[x, at_y], wg.at[x, at_y], wys.at[a], wyr.at[a], r, primary(1, a))

    def wxcopy(a, at_x):
        return to(wg.at[at_x], wg.at[at_x], wxs.at[a], wxr.at[a], r, primary(0, a))

    def scopy(q):
        return to(facc.at[q * 2 + (1 - core)], srecv.at[q], ss.at[q], sr.at[q], sib, c)

    def zcopy(d):
        return to(zsend.at[d], zrecv.at[d], zs.at[d], zr.at[d], plus(zh, d) * 2 + core, c)

    def back(h, route, a, final=False):
        at, ps_t = [], []
        for q in range(4):
            dx, dy = a * (1 - route) + q * route, q * (1 - route) + a * route
            at.append(col(h, plus(x + 4, -dx), plus(y + 4, -dy)))
            ps_t.append(pbuf[h * 16 + dx * 4 + dy, half(route)])
        hi, lo = split(jnp.concatenate(ps_t, axis=1))
        lhs = jnp.concatenate([hi, lo], axis=0)
        for d in (2, 1, 3, 0):
            row = plus(zh, d)
            for e in range(2):
                i = row * 2 + e
                rhs = jnp.concatenate([block(m, i) for m in at], axis=0)
                res = jnp.dot(lhs, rhs, preferred_element_type=F32)
                facc[i, half(route)] += (res[:H, :B] + res[H:, B:]) + (res[:H, B:] + res[H:, :B])
            if final:
                scopy(row).start()

    def arrive(h, route, a):
        dy = a * route
        for q in range(1, 4):
            sem = (h * 2 + route) * 16 + q * 4 + a
            place = pbuf.at[h * 16 + (a * (1 - route) + q * route) * 4 + q * (1 - route) + dy, half(route)]
            to(place, place, ps.at[sem], pr.at[sem], r, second(route, q)).wait_recv()

    def back_groups(h, lo, hi):
        @pl.loop(lo, hi)
        def _(g):
            n = lax.div(g, 2)
            route, a = lax.rem(g, 2), lax.rem(lax.div(n * (n + 1), 2), 4)
            arrive(h, route, a)
            back(h, route, a)

    units(0, 0)
    units(0, 1)
    units(1, 0)
    relay_sums(0, 0)
    relay_sums(0, 1)
    units(1, 1)
    relay_sums(1, 0)
    exchange(0)
    for i in range(COLS):
        facc[i] = jnp.zeros((B, B), F32)
    relay_sums(1, 1)
    ccopy.wait_recv()
    ecopy(0, 0).wait_recv()
    ecopy(0, 1).wait_recv()
    wterm[...] = middle(0)
    direct(0)
    exchange(1)
    for a in (1, 3, 2):
        relay(0, a)
    ecopy(1, 0).wait_recv()
    ecopy(1, 1).wait_recv()
    wterm[...] += middle(1)
    for a in range(1, 4):
        wacopy(a).start()
    direct(1)
    act_out[...] = acts[zl]

    back_groups(0, 0, 6)
    relay(1, 1)
    for a in range(1, 4):
        wacopy(a).wait_recv()
    wsum[...] = (wterm[pl.ds(x * 4, 4)] + wa[1]) + (wa[2] + wa[3])
    for a in range(1, 4):
        wbcopy(a).start()
    relay(1, 3)
    back_groups(0, 6, 7)
    relay(1, 2)
    back_groups(0, 7, 8)
    back_groups(1, 0, 2)
    for a in range(1, 4):
        wbcopy(a).wait_recv()
    wc[...] = (wsum[y] + wb[1]) + (wb[2] + wb[3])
    wdcopy.start()
    back_groups(1, 2, 4)
    wdcopy.wait_recv()
    wz[zh] = wc[...] + wd[...]
    for a in range(1, 4):
        wzcopy(a, zh).start()
    back_groups(1, 4, 7)
    arrive(1, 1, 2)
    back(1, 1, 2, True)

    for d in (2, 1, 3):
        q = plus(zh, d)
        scopy(q).wait_recv()
        zsend[d] = facc[q * 2 + core] + srecv[q]
        zcopy(d).start()
    scopy(zh).wait_recv()
    total = facc[r] + srecv[zh]

    for a in range(1, 4):
        wzcopy(a, plus(zh, 4 - a)).wait_recv()
    wg[x, y] = (wz[0] + wz[1]) + (wz[2] + wz[3])
    for a in range(1, 4):
        wycopy(a, y).start()

    for a in range(1, 4):
        wycopy(a, plus(y, 4 - a)).wait_recv()
    for a in range(1, 4):
        wxcopy(a, x).start()
    for a in range(1, 4):
        wxcopy(a, plus(x, 4 - a)).wait_recv()
    wgrad_out[...] = wg[...].reshape(B, B)

    ccopy.wait_send()
    wdcopy.wait_send()
    xcopy(xbuf.at[r], r, 0, sib).wait_send()
    for a in range(1, 4):
        xcopy(xbuf.at[r], r, a, sib).wait_send()
        xcopy(xbuf.at[r], r, 3 + a, sib).wait_send()
        wacopy(a).wait_send()
        wbcopy(a).wait_send()
        wzcopy(a, zh).wait_send()
        wycopy(a, y).wait_send()
        wxcopy(a, x).wait_send()
    for q in range(4):
        scopy(q).wait_send()
    for h in range(2):
        for route in range(2):
            ecopy(h, route).wait_send()
            for a in range(1, 4):
                y1copy(h, route, a, 0).wait_send()
                y1copy(h, route, a, 1).wait_send()
                y2copy(h, route, a).wait_send()
            for q in range(4):
                for a in range(4):
                    if a or q:
                        pcopy(h, route, q, a).wait_send()

    for d in (1, 3, 2):
        zcopy(d).wait_recv()
        total = total + zrecv[d]
    fgrad_out[...] = total.T
    for d in range(1, 4):
        zcopy(d).wait_send()


def deliver(a, b, c, a_out, b_out, c_out):
    a_out[...] = a[...]
    b_out[...] = b[...]
    c_out[...] = c[...]


def local(features, block_values, block_rows, block_cols, live_block_count, weight, cotangent):
    vmem = pl.BlockSpec(memory_space=pltpu.VMEM)
    anywhere = pl.BlockSpec(memory_space=pl.ANY)
    dma = pltpu.SemaphoreType.DMA
    results = [jax.ShapeDtypeStruct((B, B), F32)] * 3

    def blocks(n):
        return pltpu.VMEM((n, B, B), F32)

    outs = pl.pallas_call(
        kernel,
        out_shape=results,
        in_specs=[pl.BlockSpec(memory_space=pltpu.SMEM)] + [anywhere] * 6,
        out_specs=[vmem, vmem, vmem],
        scratch_shapes=[
            pltpu.VMEM((1, SLOTS), jnp.int32),
            pltpu.VMEM((1, SLOTS), jnp.int32),
            pltpu.VMEM((B, B), F32),
            blocks(SLOTS),
            blocks(SLOTS + 1),
            pltpu.VMEM((SLOTS + 1, B, 2 * B), BF16),
            pltpu.VMEM((1, WIDE), F32),
            pltpu.VMEM((2, WIDE), jnp.int32),
            pltpu.SMEM((2, WIDE), jnp.int32),
            blocks(COLS),
            pltpu.VMEM((COLS, 2 * B, 2 * B), BF16),
            blocks(2),
            pltpu.VMEM((16, 4, H, B), F32),
            pltpu.VMEM((16, 4, H, B), F32),
            pltpu.VMEM((16, H, B), F32),
            pltpu.VMEM((16, H, B), F32),
            blocks(2),
            blocks(2),
            blocks(2),
            blocks(32),
            blocks(COLS),
            blocks(4),
            blocks(4),
            blocks(4),
            pltpu.VMEM((16, 8, B), F32),
            pltpu.VMEM((4, 4, 8, B), F32),
            pltpu.VMEM((4, 8, B), F32),
            pltpu.VMEM((4, 8, B), F32),
            pltpu.VMEM((8, B), F32),
            pltpu.VMEM((8, B), F32),
            pltpu.VMEM((4, 8, B), F32),
            pltpu.VMEM((4, 4, 8, B), F32),
            dma((5,)), dma((CHUNKS,)), dma,
            dma((7,)), dma((8,)), dma, dma,
            dma((32,)), dma((32,)), dma((16,)), dma((16,)), dma((4,)), dma((4,)),
            dma((64,)), dma((64,)), dma((4,)), dma((4,)), dma((4,)), dma((4,)),
            dma((4,)), dma((4,)), dma((4,)), dma((4,)), dma, dma,
            dma((4,)), dma((4,)), dma((4,)), dma((4,)), dma((4,)), dma((4,)),
        ],
        compiler_params=pltpu.CompilerParams(
            collective_id=0, has_side_effects=True, vmem_limit_bytes=56 * 1024 * 1024
        ),
    )(
        live_block_count, block_rows[0], block_cols[0], features[0], weight[None], cotangent[0], block_values[0, 0]
    )
    act, wgrad, fgrad = pl.pallas_call(
        deliver,
        out_shape=results,
        in_specs=[vmem] * 3,
        out_specs=[vmem] * 3,

    )(*outs)
    return act[None], wgrad, fgrad[None]


def solution(mesh):
    in_specs = (
        P("col", "row", None),
        P("row", "col", None, None, None),
        P("row", "col", None),
        P("row", "col", None),
        P("row", "col"),
        P(),
        P("row", "col", None),
    )
    out_specs = (P("row", "col", None), P(), P("col", "row", None))
    return jax.shard_map(local, mesh=mesh, in_specs=in_specs, out_specs=out_specs, check_vma=False)
```
